256 devices in a mesh: region: 32 (over z, y), tm: 8 (over x, core).
Axes of the slice: x: 4, y: 4, z: 8, core: 2. Of those that a mesh axis runs over, the one named last changes fastest.
Arguments:
- signal: bfloat16 [32, 32, 131072], P('tm', None, 'region'), may hold values from -6 to 6
- time_weight: bfloat16 [2, 64, 32], replicated, may hold values from -0.75 to 0.75
- time_bias: float32 [64], replicated, may hold values from -3 to 3
- mix_weight: bfloat16 [32, 160], replicated, may hold values from -1 to 1
- mix_bias: float32 [32], replicated, may hold values from -3 to 3
- tile_values: bfloat16 [32, 96, 128, 128], P('region'), may hold values from -1 to 1
- tile_rows: int32 [32, 96], P('region'), may hold values from 0 to 31, as said below
- tile_cols: int32 [32, 96], P('region'), may hold values from 0 to 39, as said below
- tile_count: int32 [32], P('region'), may hold values from 34 to 96, as said below
Outputs:
- layer_out: bfloat16 [32, 32, 131072], P('tm', None, 'region')
The draws below stay inside these ranges and needn't reach their ends.
Inputs may be any that keep to these rules, and one draw needn't show every extreme that they name: `tile_count`: some region has all 96 slots live in every draw. `tile_rows`: slot s < 32 holds row tile s. `tile_cols`: values under 4 name the previous region's last 4 tiles, values of 36 or more the next region's first 4 tiles; the first region never names the previous one, the last never the next one. Slot s < 32 names s + 4.
All inputs are finite; a program needn't handle non-finite values.
Results may differ from the reference program's by a relative error of at most 0.0045.
Values may be sent and summed in bfloat16 or wider, within the bound.
A program may use at most 192 MiB of HBM per device.

```python
from functools import partial
import jax
import jax.numpy as jnp
from jax import lax

CH = 32
TILE = 128
DILATION_DAYS = 4
HB = 4
RT = 32
MAXT = 96
REGIONS = 32
DAYS = 32
PARCELS = 131072


def tile_plan(key):
    keys = jax.random.split(key, 8)
    span = 2 * RT - 1
    first = jax.random.randint(keys[0], (REGIONS,), 0, span)
    second = jax.random.randint(keys[1], (REGIONS,), 0, span)
    third = jax.random.randint(keys[2], (REGIONS,), 0, span)
    extra = jnp.minimum(jnp.minimum(first, second), third) + 2
    fullest = jax.random.randint(keys[3], (), 0, REGIONS)
    region = jnp.arange(REGIONS, dtype=jnp.int32)
    extra = jnp.where(region == fullest, 2 * RT, extra)
    live_count = (RT + extra).astype(jnp.int32)
    slot_ids = jnp.arange(MAXT, dtype=jnp.int32)[None, :]
    regcol = region[:, None]
    free_rows = jax.random.randint(keys[4], (REGIONS, MAXT), 0, RT)
    rows = jnp.where(slot_ids < RT, slot_ids, free_rows)
    free_cols = jax.random.randint(keys[5], (REGIONS, MAXT), 0, RT + 2 * HB)
    free_cols = jnp.where((regcol == 0) & (free_cols < HB), free_cols + HB, free_cols)
    free_cols = jnp.where((regcol == REGIONS - 1) & (free_cols >= RT + HB), free_cols - HB, free_cols)
    prev_col = jax.random.randint(keys[6], (REGIONS, 1), 0, HB)
    prev_col = jnp.where(regcol == 1, 0, prev_col)
    prev_col = jnp.where(regcol == 0, prev_col + HB, prev_col)
    next_col = RT + HB + jax.random.randint(keys[7], (REGIONS, 1), 0, HB)
    next_col = jnp.where(regcol == 0, RT + 2 * HB - 1, next_col)
    next_col = jnp.where(regcol == REGIONS - 1, next_col - HB, next_col)
    cols = jnp.where(slot_ids < RT, slot_ids + HB, jnp.where(slot_ids == RT, prev_col, jnp.where(slot_ids == RT + 1, next_col, free_cols)))
    return (live_count, rows.astype(jnp.int32), cols.astype(jnp.int32))


def draw_tile_count(key, part):
    plan = tile_plan(key)
    return plan[0]


def draw_tile_rows(key, part):
    plan = tile_plan(key)
    return plan[1]


def draw_tile_cols(key, part):
    plan = tile_plan(key)
    return plan[2]


def steps_of(rng, dims, shards, smallest, largest):
    def one(dim, blocks):
        steps = jax.random.uniform(jax.random.fold_in(jax.random.fold_in(rng, 6), dim), (blocks,), jnp.float32, smallest / len(shards), largest / len(shards))
        return jnp.repeat(jnp.exp(steps), dims[dim] // blocks).reshape((-1,) + (1,) * (len(dims) - dim - 1))

    gain = one(*shards[0])
    for cut in shards[1:]:
        gain = gain * one(*cut)
    return gain


def centred(own_key, extent, width, reach, pieces=(), kind=jnp.bfloat16):
    loudness = steps_of(own_key, extent, pieces, -0.22, 0.18) if pieces else 1.0
    array = jax.random.normal(own_key, extent, jnp.float32) * width * loudness
    return jnp.minimum(jnp.maximum(array, -reach), reach).astype(kind)


def setup_inputs(seed: int = 0) -> dict:
    arg_keys = jax.random.split(jax.random.key(seed), 10)
    return {
        "signal": centred(arg_keys[0], (DAYS, CH, PARCELS), 1.0, 6.0, ((0, 8), (2, 32))),
        "time_weight": centred(arg_keys[1], (2, 2 * CH, CH), (2 * CH) ** -0.5, 0.75),
        "time_bias": centred(arg_keys[2], (2 * CH,), 0.5, 3.0, (), jnp.float32),
        "mix_weight": centred(arg_keys[3], (CH, 5 * CH), CH ** -0.5, 1.0),
        "mix_bias": centred(arg_keys[4], (CH,), 0.5, 3.0, (), jnp.float32),
        "tile_values": centred(arg_keys[5], (REGIONS, MAXT, TILE, TILE), 0.0625, 1.0, ((0, 32),)),
        "tile_rows": draw_tile_rows(jax.random.fold_in(arg_keys[9], 71), 0),
        "tile_cols": draw_tile_cols(jax.random.fold_in(arg_keys[9], 71), 0),
        "tile_count": draw_tile_count(jax.random.fold_in(arg_keys[9], 71), 0),
    }


def gate_day(time_weight, time_bias, day_pair):
    lagged_day, current_day = day_pair
    preact = jnp.dot(time_weight[0], lagged_day, preferred_element_type=jnp.float32)
    preact = preact + jnp.dot(time_weight[1], current_day, preferred_element_type=jnp.float32)
    preact = preact + time_bias[:, None]
    return (jnp.tanh(preact[:CH]) * jax.nn.sigmoid(preact[CH:])).astype(jnp.bfloat16)


def tile_sweep(source, tile_values, tile_rows, tile_cols, tile_count, transposed):
    row_total, parcel_nodes = source.shape
    tile_total = parcel_nodes // TILE
    blocks = source.reshape(row_total, tile_total, TILE)
    padded = jnp.pad(blocks, ((0, 0), (HB, HB), (0, 0)))
    slot_ids = jnp.arange(MAXT, dtype=jnp.int32)

    def visit_region(running, region_item):
        values, rows, cols, live_count, region = region_item
        row_index = (region * RT + HB + rows).astype(jnp.int32)
        col_index = (region * RT + cols).astype(jnp.int32)
        if transposed:
            take_index, put_index, equation = row_index, col_index, "mgi,gij->mgj"
        else:
            take_index, put_index, equation = col_index, row_index, "mgj,gij->mgi"
        panels = jnp.take(padded, take_index, axis=1).astype(jnp.float32)
        products = jnp.einsum(equation, panels, values.astype(jnp.float32))
        live_mask = (slot_ids < live_count)[None, :, None]
        products = jnp.where(live_mask, products, jnp.zeros_like(products))
        return running.at[:, put_index].add(products), None

    zero_sum = jnp.zeros((row_total, tile_total + 2 * HB, TILE), jnp.float32)
    regions = jnp.arange(REGIONS, dtype=jnp.int32)
    running, _ = lax.scan(visit_region, zero_sum, (tile_values, tile_rows, tile_cols, tile_count, regions))
    return running[:, HB:HB + tile_total].reshape(row_total, parcel_nodes)


def mix_day(mix_weight, mix_bias, day_items):
    signal_day = day_items[0]
    running = signal_day.astype(jnp.float32) + mix_bias[:, None]
    for branch_index in range(5):
        weight_part = mix_weight[:, branch_index * CH:(branch_index + 1) * CH]
        running = running + jnp.dot(weight_part, day_items[branch_index + 1], preferred_element_type=jnp.float32)
    return running.astype(jnp.bfloat16)


def reference(signal, time_weight, time_bias, mix_weight, mix_bias, tile_values, tile_rows, tile_cols, tile_count):
    total_days, channel_count, parcel_nodes = signal.shape
    lagged_signal = jnp.concatenate([jnp.zeros((DILATION_DAYS, channel_count, parcel_nodes), jnp.bfloat16), signal[:total_days - DILATION_DAYS]], 0)
    hidden = lax.map(partial(gate_day, time_weight, time_bias), (lagged_signal, signal))
    flattened = hidden.reshape(total_days * channel_count, parcel_nodes)
    fwd_one = tile_sweep(flattened, tile_values, tile_rows, tile_cols, tile_count, False).astype(jnp.bfloat16)
    bwd_one = tile_sweep(flattened, tile_values, tile_rows, tile_cols, tile_count, True).astype(jnp.bfloat16)
    fwd_two = tile_sweep(fwd_one, tile_values, tile_rows, tile_cols, tile_count, False).astype(jnp.bfloat16)
    bwd_two = tile_sweep(bwd_one, tile_values, tile_rows, tile_cols, tile_count, True).astype(jnp.bfloat16)
    shape = (total_days, channel_count, parcel_nodes)
    branches = (signal, hidden, fwd_one.reshape(shape), fwd_two.reshape(shape), bwd_one.reshape(shape), bwd_two.reshape(shape))
    return lax.map(partial(mix_day, mix_weight, mix_bias), branches)
```

```python
import jax
import jax.numpy as jnp
from jax import lax
from jax.experimental import pallas as pl
from jax.experimental.pallas import tpu as pltpu
from jax.sharding import PartitionSpec as P

HB = 4
DAYS = 4
CH = 32
T = 128
ROWS = DAYS * CH
SLOTS = 96
RT = 32
EXTRA = SLOTS - RT
CHUNK = 4
CHUNKS = RT // CHUNK
MESH = pl.DeviceIdType.MESH
F32 = jnp.float32
BF16 = jnp.bfloat16
I32 = jnp.int32


def iota(shape, dim):
    return lax.broadcasted_iota(I32, shape, dim)


def nn(a, b):
    return jnp.dot(a, b, preferred_element_type=F32)


def nt(a, b):
    return lax.dot_general(a, b, (((1,), (1,)), ((), ())), preferred_element_type=F32)


def segments(keys, takes):
    square = (T, T)
    slot_row = iota(square, 0)
    slot_col = iota(square, 1)
    by_col = jnp.broadcast_to(keys, square)
    by_row = by_col.T
    take_row = jnp.broadcast_to(takes, square).T
    earlier_same = ((by_col == by_row) & (slot_col < slot_row)).astype(I32)
    lower = (by_col < by_row).astype(I32)
    rank = jnp.sum(earlier_same + lower, axis=1, keepdims=True)
    keep = (jnp.sum(earlier_same, axis=1, keepdims=True) > 0).astype(I32)
    at = rank == slot_col
    zero = jnp.zeros(square, I32)
    perm = jnp.sum(jnp.where(at, jnp.minimum(slot_row, SLOTS - 1), zero), axis=0, keepdims=True)
    take = jnp.sum(jnp.where(at, take_row, zero), axis=0, keepdims=True)
    kept = jnp.sum(jnp.where(at, jnp.broadcast_to(keep, square), zero), axis=0, keepdims=True)
    upto = jnp.sum((by_row <= slot_col).astype(I32), axis=0, keepdims=True)
    count = jnp.sum((by_row == slot_col).astype(I32), axis=0, keepdims=True)
    last = jnp.where(count > 0, upto, 0)
    return perm, take, kept, last


def kernel(
    signal_ref,
    time_weight_ref,
    time_bias_ref,
    mix_weight_ref,
    mix_bias_ref,
    tiles_hbm,
    rows_ref,
    cols_ref,
    count_ref,
    out_hbm,
    cur,
    lag,
    tiles,
    hidden,
    fwd,
    bwd,
    sums_f,
    sums_b,
    rim_out,
    rim_in,
    rim_out2,
    rim_in2,
    out,
    conv_w,
    mix_w,
    table_v,
    table,
    local_sem,
    x_send,
    x_recv,
    r_send,
    r_recv,
    out_sem,
):
    region = lax.axis_index("region")
    tm = lax.axis_index("tm")
    regions = lax.axis_size("region")
    tms = lax.axis_size("tm")
    above = (lax.rem(region + 1, regions), tm)
    below = (lax.rem(region + regions - 1, regions), tm)
    later = (region, lax.rem(tm + 1, tms))
    earlier = (region, lax.rem(tm + tms - 1, tms))

    barrier = pltpu.get_barrier_semaphore()
    for peer in (above, below, later, earlier):
        pl.semaphore_signal(barrier, inc=1, device_id=peer, device_id_type=MESH)

    load_signal = pltpu.make_async_copy(signal_ref, cur, local_sem.at[0])
    load_signal.start()
    load_tiles = pltpu.make_async_copy(tiles_hbm, tiles, local_sem.at[1])
    load_tiles.start()
    pl.semaphore_wait(barrier, 4)

    def chunk_of(turn):
        return jnp.where(turn == 0, 0, jnp.where(turn == 1, CHUNKS - 1, turn - 1))

    def columns(chunk):
        return pl.ds(pl.multiple_of(chunk * (CHUNK * T), CHUNK * T), CHUNK * T)

    def shift(turn):
        where = columns(chunk_of(turn))
        return pltpu.make_async_remote_copy(
            src_ref=signal_ref.at[:, where],
            dst_ref=lag.at[:, where],
            send_sem=x_send.at[turn],
            recv_sem=x_recv.at[turn],
            device_id=later,
            device_id_type=MESH,
        )

    def start_shift(turn, carry):
        shift(turn).start()
        return carry

    lax.fori_loop(0, CHUNKS, start_shift, 0)

    lane = iota((1, T), 1)
    pad = jnp.zeros((1, T - SLOTS), I32)
    rows = jnp.concatenate([rows_ref[...], pad], axis=1)
    cols = jnp.concatenate([cols_ref[...], pad], axis=1)
    live = (lane >= RT) & (lane < count_ref[0])
    far = jnp.full((1, T), 2 * T, I32)
    perm_f, take_f, keep_f, last_f = segments(jnp.where(live, rows, far), cols)
    perm_b, take_b, keep_b, last_b = segments(jnp.where(live, cols, far), rows)
    table_v[...] = jnp.concatenate(
        [perm_f, take_f, keep_f, last_f, perm_b, take_b, keep_b, last_b], axis=0
    )
    to_scalars = pltpu.make_async_copy(table_v, table, local_sem.at[2])
    to_scalars.start()

    spread = (lax.rem(iota((ROWS, CH), 0), CH) == iota((ROWS, CH), 1)).astype(BF16)
    same_day = iota((ROWS, ROWS), 0) // CH == iota((ROWS, ROWS), 1) // CH
    for part in range(2):
        scale = 1.0 if part == 0 else 0.5
        for tap in range(2):
            block = time_weight_ref[tap, part * CH : (part + 1) * CH, :]
            wide = nt(nn(spread, block).astype(BF16), spread)
            conv_w[part * ROWS : (part + 1) * ROWS, tap * ROWS : (tap + 1) * ROWS] = jnp.where(
                same_day, wide * scale, 0.0
            ).astype(BF16)
    tall_mix = nn(spread, mix_weight_ref[...]).astype(BF16)
    for branch in range(5):
        pick = (
            iota((5 * CH, ROWS), 0) == branch * CH + lax.rem(iota((5 * CH, ROWS), 1), CH)
        ).astype(BF16)
        mix_w[:, branch * ROWS : (branch + 1) * ROWS] = jnp.where(
            same_day, nn(tall_mix, pick), 0.0
        ).astype(BF16)
    channel = lax.rem(iota((ROWS, 1), 0), CH)

    def column_of(values, first):
        width = values.shape[1]
        hit = iota((ROWS, width), 1) == channel + first
        return jnp.sum(jnp.where(hit, jnp.broadcast_to(values, (ROWS, width)), 0.0), 1, keepdims=True)

    time_bias = time_bias_ref[...].reshape(1, 2 * CH)
    bias_filter = column_of(time_bias, 0)
    bias_gate = column_of(time_bias, CH) * 0.5
    bias_mix = column_of(mix_bias_ref[...].reshape(1, CH), 0)

    sums_f[0] = jnp.zeros((T, T), F32)
    sums_b[0] = jnp.zeros((T, T), F32)

    def to_region(src, dst, index, peer):
        return pltpu.make_async_remote_copy(
            src_ref=src,
            dst_ref=dst,
            send_sem=r_send.at[index],
            recv_sem=r_recv.at[index],
            device_id=peer,
            device_id_type=MESH,
        )

    halo_low = to_region(hidden.at[pl.ds(HB, HB)], hidden.at[pl.ds(HB + RT, HB)], 0, below)
    halo_high = to_region(hidden.at[pl.ds(RT, HB)], hidden.at[pl.ds(0, HB)], 1, above)
    rim_low = to_region(rim_out.at[pl.ds(0, HB)], rim_in.at[pl.ds(HB, HB)], 2, below)
    rim_high = to_region(rim_out.at[pl.ds(HB, HB)], rim_in.at[pl.ds(0, HB)], 3, above)
    fwd_low = to_region(fwd.at[pl.ds(HB, HB)], fwd.at[pl.ds(HB + RT, HB)], 4, below)
    fwd_high = to_region(fwd.at[pl.ds(RT, HB)], fwd.at[pl.ds(0, HB)], 5, above)
    rim2_low = to_region(rim_out2.at[pl.ds(0, HB)], rim_in2.at[pl.ds(HB, HB)], 6, below)
    rim2_high = to_region(rim_out2.at[pl.ds(HB, HB)], rim_in2.at[pl.ds(0, HB)], 7, above)

    load_signal.wait()
    first_block = jnp.where(tm == 0, 0.0, 1.0).astype(BF16)

    def gate(turn, carry):
        chunk = chunk_of(turn)
        where = columns(chunk)
        shift(turn).wait_recv()
        pre = nn(conv_w[:, :ROWS], lag[:, where] * first_block) + nn(conv_w[:, ROWS:], cur[:, where])
        value = jnp.tanh(pre[:ROWS] + bias_filter) * (0.5 + 0.5 * jnp.tanh(pre[ROWS:] + bias_gate))
        value = value.astype(BF16)
        for tile in range(CHUNK):
            hidden[HB + chunk * CHUNK + tile] = value[:, tile * T : (tile + 1) * T]
        return carry

    gate(0, 0)
    halo_low.start()
    gate(1, 0)
    halo_high.start()
    lax.fori_loop(2, CHUNKS, gate, 0)
    to_scalars.wait()
    load_tiles.wait()

    def extras_f(source):
        def add(place, running):
            product = nt(source[table[1, place]], tiles[table[0, place]])
            running = jnp.where(table[2, place] > 0, running, 0.0) + product
            sums_f[place + 1] = running
            return running

        lax.fori_loop(0, EXTRA, add, jnp.zeros((T, T), F32), unroll=4)

    def extras_b(source, base):
        def add(place, running):
            product = nn(source[table[5, place] + base], tiles[table[4, place]])
            running = jnp.where(table[6, place] > 0, running, 0.0) + product
            sums_b[place + 1] = running
            return running

        lax.fori_loop(0, EXTRA, add, jnp.zeros((T, T), F32), unroll=4)

    def rims(target):
        def fill(tile, carry):
            target[tile] = sums_b[table[7, tile]].astype(BF16)
            target[HB + tile] = sums_b[table[7, HB + RT + tile]].astype(BF16)
            return carry

        lax.fori_loop(0, HB, fill, 0)

    def forward(source, tile):
        return nt(source[HB + tile], tiles[tile]) + sums_f[table[3, tile]]

    def backward(source, base, tile):
        return nn(source[base + tile], tiles[tile]) + sums_b[table[7, HB + tile]]

    halo_low.wait()
    halo_high.wait()
    extras_b(hidden, HB)
    rims(rim_out)
    rim_low.start()
    rim_high.start()
    extras_f(hidden)

    def fwd_tile(tile, carry):
        fwd[HB + tile] = forward(hidden, tile).astype(BF16)
        return carry

    lax.fori_loop(0, HB, fwd_tile, 0)
    fwd_low.start()
    lax.fori_loop(RT - HB, RT, fwd_tile, 0)
    fwd_high.start()
    lax.fori_loop(HB, RT - HB, fwd_tile, 0, unroll=4)

    def bwd_tile(tile, carry):
        bwd[tile] = backward(hidden, HB, tile).astype(BF16)
        return carry

    lax.fori_loop(HB, RT - HB, bwd_tile, 0, unroll=4)
    rim_low.wait()
    rim_high.wait()

    def bwd_rim(tile, carry):
        low, high = tile, RT - HB + tile
        bwd[low] = (backward(hidden, HB, low) + rim_in[tile].astype(F32)).astype(BF16)
        bwd[high] = (backward(hidden, HB, high) + rim_in[HB + tile].astype(F32)).astype(BF16)
        return carry

    lax.fori_loop(0, HB, bwd_rim, 0)

    extras_b(bwd, 0)
    rims(rim_out2)
    rim2_low.start()
    rim2_high.start()
    fwd_low.wait()
    fwd_high.wait()
    extras_f(fwd)

    def mixed(tile, rim):
        two = backward(bwd, 0, tile)
        if rim is not None:
            two = two + rim.astype(F32)
        blocks = jnp.concatenate(
            [
                hidden[HB + tile],
                fwd[HB + tile],
                forward(fwd, tile).astype(BF16),
                bwd[tile],
                two.astype(BF16),
            ],
            axis=0,
        )
        where = pl.ds(pl.multiple_of(tile * T, T), T)
        total = nn(mix_w[...], blocks) + cur[:, where].astype(F32) + bias_mix
        out[:, where] = total.astype(BF16)

    def mix_inner(tile, carry):
        mixed(tile, None)
        return carry

    def store(first, count, index):
        where = pl.ds(first * T, count * T)
        return pltpu.make_async_copy(out.at[:, where], out_hbm.at[:, where], out_sem.at[index])

    lax.fori_loop(HB, RT - HB, mix_inner, 0, unroll=2)
    inner_store = store(HB, RT - 2 * HB, 0)
    inner_store.start()
    rim2_low.wait()
    rim2_high.wait()

    def mix_rim(tile, carry):
        mixed(tile, rim_in2[tile])
        mixed(RT - HB + tile, rim_in2[HB + tile])
        return carry

    lax.fori_loop(0, HB, mix_rim, 0)
    low_store = store(0, HB, 1)
    high_store = store(RT - HB, HB, 2)
    low_store.start()
    high_store.start()

    def end_shift(turn, carry):
        shift(turn).wait_send()
        return carry

    lax.fori_loop(0, CHUNKS, end_shift, 0)
    inner_store.wait()
    low_store.wait()
    high_store.wait()


def body(
    signal,
    time_weight,
    time_bias,
    mix_weight,
    mix_bias,
    tile_values,
    tile_rows,
    tile_cols,
    tile_count,
):
    width = signal.shape[2]
    anywhere = pl.BlockSpec(memory_space=pl.ANY)
    vmem = pl.BlockSpec(memory_space=pltpu.VMEM)
    smem = pl.BlockSpec(memory_space=pltpu.SMEM)
    panel = pltpu.VMEM((ROWS, width), BF16)
    result = pl.pallas_call(
        kernel,
        out_shape=jax.ShapeDtypeStruct((ROWS, width), BF16),
        in_specs=[anywhere, vmem, vmem, vmem, vmem, anywhere, vmem, vmem, smem],
        out_specs=anywhere,
        scratch_shapes=[
            panel,
            panel,
            pltpu.VMEM((SLOTS, T, T), BF16),
            pltpu.VMEM((RT + 2 * HB, ROWS, T), BF16),
            pltpu.VMEM((RT + 2 * HB, ROWS, T), BF16),
            pltpu.VMEM((RT, ROWS, T), BF16),
            pltpu.VMEM((EXTRA + 1, ROWS, T), F32),
            pltpu.VMEM((EXTRA + 1, ROWS, T), F32),
            pltpu.VMEM((2 * HB, ROWS, T), BF16),
            pltpu.VMEM((2 * HB, ROWS, T), BF16),
            pltpu.VMEM((2 * HB, ROWS, T), BF16),
            pltpu.VMEM((2 * HB, ROWS, T), BF16),
            panel,
            pltpu.VMEM((2 * ROWS, 2 * ROWS), BF16),
            pltpu.VMEM((ROWS, 5 * ROWS), BF16),
            pltpu.VMEM((8, T), I32),
            pltpu.SMEM((8, T), I32),
            pltpu.SemaphoreType.DMA((3,)),
            pltpu.SemaphoreType.DMA((CHUNKS,)),
            pltpu.SemaphoreType.DMA((CHUNKS,)),
            pltpu.SemaphoreType.DMA((8,)),
            pltpu.SemaphoreType.DMA((8,)),
            pltpu.SemaphoreType.DMA((3,)),
        ],
        compiler_params=pltpu.CompilerParams(
            collective_id=0, has_side_effects=True, vmem_limit_bytes=56 * 2**20
        ),
    )(
        signal.reshape(ROWS, width),
        time_weight,
        time_bias,
        mix_weight,
        mix_bias,
        tile_values[0],
        tile_rows,
        tile_cols,
        tile_count,
    )
    return result.reshape(signal.shape)


def solution(mesh):
    placed = (
        P("tm", None, "region"),
        P(),
        P(),
        P(),
        P(),
        P("region", None, None, None),
        P("region", None),
        P("region", None),
        P("region"),
    )
    return jax.shard_map(
        body, mesh=mesh, in_specs=placed, out_specs=P("tm", None, "region"), check_vma=False
    )
```

```python
import jax
import jax.numpy as jnp
from jax import lax
from jax.experimental import pallas as pl
from jax.experimental.pallas import tpu as pltpu
from jax.sharding import PartitionSpec as P

HB = 4
DAYS = 4
CH = 32
T = 128
GROUPS = 1
ROWS = DAYS * CH // GROUPS
SLOTS = 96
RT = 32
EXTRA = SLOTS - RT
CHUNK = 8 if GROUPS == 2 else 4
PAIR = 2
UNROLL = 64
INNER = 12
MIXED = 4
CHUNKS = RT // CHUNK
MESH = pl.DeviceIdType.MESH
F32 = jnp.float32
BF16 = jnp.bfloat16
I32 = jnp.int32


def iota(shape, dim):
    return lax.broadcasted_iota(I32, shape, dim)


def nn(a, b):
    return jnp.dot(a, b, preferred_element_type=F32)


def segments(keys, takes):
    square = (T, T)
    slot_row = iota(square, 0)
    slot_col = iota(square, 1)
    by_col = jnp.broadcast_to(keys, square)
    by_row = by_col.T
    take_row = jnp.broadcast_to(takes, square).T
    earlier_same = ((by_col == by_row) & (slot_col < slot_row)).astype(I32)
    lower = (by_col < by_row).astype(I32)
    rank = jnp.sum(earlier_same + lower, axis=1, keepdims=True)
    keep = (jnp.sum(earlier_same, axis=1, keepdims=True) > 0).astype(I32)
    at = rank == slot_col
    zero = jnp.zeros(square, I32)
    perm = jnp.sum(jnp.where(at, jnp.minimum(slot_row, SLOTS - 1), zero), axis=0, keepdims=True)
    take = jnp.sum(jnp.where(at, take_row, zero), axis=0, keepdims=True)
    kept = jnp.sum(jnp.where(at, jnp.broadcast_to(keep, square), zero), axis=0, keepdims=True)
    upto = jnp.sum((by_row <= slot_col).astype(I32), axis=0, keepdims=True)
    count = jnp.sum((by_row == slot_col).astype(I32), axis=0, keepdims=True)
    last = jnp.where(count > 0, upto, 0)
    return perm, take, kept, last


def kernel(
    signal_ref,
    time_weight_hbm,
    time_bias_hbm,
    mix_weight_hbm,
    mix_bias_hbm,
    tiles_hbm,
    rows_hbm,
    cols_hbm,
    count_hbm,
    out_ref,
    cur,
    lag,
    tiles,
    tiles_t,
    hidden,
    fwd,
    bwd,
    sums_f,
    sums_b,
    rim_out,
    rim_in,
    rim_out2,
    rim_in2,
    out,
    conv_w,
    mix_w,
    time_weight_ref,
    time_bias_ref,
    mix_weight_ref,
    mix_bias_ref,
    rows_ref,
    cols_ref,
    count_ref,
    table_v,
    table,
    local_sem,
    x_send,
    x_recv,
    r_send,
    r_recv,
    out_sem,
):
    region = lax.axis_index("region")
    tm = lax.axis_index("tm")
    regions = lax.axis_size("region")
    tms = lax.axis_size("tm")
    above = (lax.rem(region + 1, regions), tm)
    below = (lax.rem(region + regions - 1, regions), tm)
    later = (region, lax.rem(tm + 1, tms))
    earlier = (region, lax.rem(tm + tms - 1, tms))

    barrier = pltpu.get_barrier_semaphore()
    for peer in (later, earlier, above, below):
        pl.semaphore_signal(barrier, inc=1, device_id=peer, device_id_type=MESH)

    loads = [
        pltpu.make_async_copy(src, dst, local_sem.at[index])
        for index, (src, dst) in enumerate(
            [
                (count_hbm, count_ref),
                (rows_hbm, rows_ref),
                (cols_hbm, cols_ref),
                (time_weight_hbm, time_weight_ref),
                (time_bias_hbm, time_bias_ref),
                (mix_weight_hbm, mix_weight_ref),
                (mix_bias_hbm, mix_bias_ref),
                (signal_ref, cur),
                (tiles_hbm, tiles),
            ]
        )
    ]
    for load in loads:
        load.start()
    pl.semaphore_wait(barrier, 4)

    def columns(chunk):
        return pl.ds(chunk * (CHUNK * T), CHUNK * T)

    def shift(group, chunk):
        where = (pl.ds(group * ROWS, ROWS), columns(chunk))
        index = group * CHUNKS + chunk
        return pltpu.make_async_remote_copy(
            src_ref=signal_ref.at[where],
            dst_ref=lag.at[where],
            send_sem=x_send.at[index],
            recv_sem=x_recv.at[index],
            device_id=later,
            device_id_type=MESH,
        )

    order = [0, CHUNKS - 1] + list(range(1, CHUNKS - 1))
    for group in range(GROUPS):
        for chunk in order:
            shift(group, chunk).start()
    for load in loads[:7]:
        load.wait()

    spread = (lax.rem(iota((ROWS, CH), 0), CH) == iota((ROWS, CH), 1)).astype(BF16)
    same_day = iota((ROWS, ROWS), 0) // CH == iota((ROWS, ROWS), 1) // CH
    has_earlier = jnp.where(tm == 0, 0.0, 1.0)
    for part in range(2):
        tall = [nn(spread, time_weight_ref[tap]).astype(BF16) for tap in range(2)]
        pick = (
            iota((2 * CH, ROWS), 0) == part * CH + lax.rem(iota((2 * CH, ROWS), 1), CH)
        ).astype(BF16)
        for tap in range(2):
            wide = nn(tall[tap], pick).T * (1.0 if part == 0 else 0.5)
            if tap == 0:
                wide = wide * has_earlier
            conv_w[part * ROWS : (part + 1) * ROWS, tap * ROWS : (tap + 1) * ROWS] = jnp.where(
                same_day, wide, 0.0
            ).astype(BF16)
    tall_mix = nn(spread, mix_weight_ref[...]).astype(BF16)
    for branch in range(5):
        pick = (
            iota((5 * CH, ROWS), 0) == branch * CH + lax.rem(iota((5 * CH, ROWS), 1), CH)
        ).astype(BF16)
        mix_w[:, branch * ROWS : (branch + 1) * ROWS] = jnp.where(
            same_day, nn(tall_mix, pick), 0.0
        ).astype(BF16)
    channel = lax.rem(iota((ROWS, 1), 0), CH)

    def column_of(values, first):
        width = values.shape[1]
        hit = iota((ROWS, width), 1) == channel + first
        return jnp.sum(jnp.where(hit, jnp.broadcast_to(values, (ROWS, width)), 0.0), 1, keepdims=True)

    time_bias = time_bias_ref[...].reshape(1, 2 * CH)
    bias_filter = column_of(time_bias, 0)
    bias_gate = column_of(time_bias, CH) * 0.5
    bias_mix = column_of(mix_bias_ref[...].reshape(1, CH), 0)
    loads[7].wait()

    def to_region(src, dst, index, peer):
        return pltpu.make_async_remote_copy(
            src_ref=src,
            dst_ref=dst,
            send_sem=r_send.at[index],
            recv_sem=r_recv.at[index],
            device_id=peer,
            device_id_type=MESH,
        )

    first_tiles, last_tiles = pl.ds(HB, HB), pl.ds(RT, HB)
    from_below, from_above = pl.ds(0, HB), pl.ds(HB + RT, HB)
    rim_first, rim_last = pl.ds(0, HB), pl.ds(HB, HB)
    halo, rim, edge, rim2 = [], [], [], []
    for g in range(GROUPS):
        base = 8 * g
        halo.append(
            (
                to_region(hidden[g].at[first_tiles], hidden[g].at[from_above], base, below),
                to_region(hidden[g].at[last_tiles], hidden[g].at[from_below], base + 1, above),
            )
        )
        rim.append(
            (
                to_region(rim_out[g].at[rim_first], rim_in[g].at[rim_last], base + 2, below),
                to_region(rim_out[g].at[rim_last], rim_in[g].at[rim_first], base + 3, above),
            )
        )
        edge.append(
            (
                to_region(fwd[g].at[first_tiles], fwd[g].at[from_above], base + 4, below),
                to_region(fwd[g].at[last_tiles], fwd[g].at[from_below], base + 5, above),
            )
        )
        rim2.append(
            (
                to_region(rim_out2[g].at[rim_first], rim_in2[g].at[rim_last], base + 6, below),
                to_region(rim_out2[g].at[rim_last], rim_in2[g].at[rim_first], base + 7, above),
            )
        )

    def gate(group, chunk):
        shift(group, chunk).wait_recv()
        rows_here = pl.ds(group * ROWS, ROWS)

        def part(index, carry):
            first = chunk * CHUNK + index * PAIR
            where = pl.ds(pl.multiple_of(first * T, PAIR * T), PAIR * T)
            days = jnp.concatenate([lag[rows_here, where], cur[rows_here, where]], axis=0)
            pre = nn(conv_w[...], days)
            value = jnp.tanh(pre[:ROWS] + bias_filter) * (
                0.5 + 0.5 * jnp.tanh(pre[ROWS:] + bias_gate)
            )
            value = value.astype(BF16)
            for tile in range(PAIR):
                hidden[group][HB + first + tile] = value[:, tile * T : (tile + 1) * T]
            return carry

        lax.fori_loop(0, CHUNK // PAIR, part, 0, unroll=CHUNK // PAIR)

    def outer_gates(group):
        gate(group, 0)
        halo[group][0].start()
        gate(group, CHUNKS - 1)
        halo[group][1].start()

    def inner_gates(group):
        for chunk in range(1, CHUNKS - 1):
            gate(group, chunk)

    def extras(source, base, values, sums, first):
        def add(place, running):
            product = nn(source[table[first + 1, place] + base], values[table[first, place]])
            running = jnp.where(table[first + 2, place] > 0, running, 0.0) + product
            sums[place + 1] = running
            return running

        lax.fori_loop(0, EXTRA, add, jnp.zeros((ROWS, T), F32), unroll=UNROLL)

    def extras_f(g, source):
        extras(source, 0, tiles_t, sums_f[g], 0)

    def extras_b(g, source, base):
        extras(source, base, tiles, sums_b[g], 4)

    def rims(g, target):
        def fill(tile, carry):
            target[tile] = sums_b[g][table[7, tile]].astype(BF16)
            target[HB + tile] = sums_b[g][table[7, HB + RT + tile]].astype(BF16)
            return carry

        lax.fori_loop(0, HB, fill, 0, unroll=HB)

    def forward(g, source, tile):
        return nn(source[HB + tile], tiles_t[tile]) + sums_f[g][table[3, tile]]

    def backward(g, source, base, tile):
        return nn(source[base + tile], tiles[tile]) + sums_b[g][table[7, HB + tile]]

    def hop_one(g):
        halo[g][0].wait()
        halo[g][1].wait()
        extras_b(g, hidden[g], HB)
        rims(g, rim_out[g])
        rim[g][0].start()
        rim[g][1].start()
        extras_f(g, hidden[g])

        def fwd_tile(tile, carry):
            fwd[g][HB + tile] = forward(g, hidden[g], tile).astype(BF16)
            return carry

        def fwd_rim(tile, carry):
            return fwd_tile(RT - HB + tile, fwd_tile(tile, carry))

        lax.fori_loop(0, HB, fwd_rim, 0, unroll=HB)
        edge[g][0].start()
        edge[g][1].start()

        def inner(tile, carry):
            bwd[g][tile] = backward(g, hidden[g], HB, tile).astype(BF16)
            return fwd_tile(tile, carry)

        lax.fori_loop(HB, RT - HB, inner, 0, unroll=INNER)

    def backward_two(g):
        rim[g][0].wait()
        rim[g][1].wait()

        def bwd_rim(tile, carry):
            low, high = tile, RT - HB + tile
            bwd[g][low] = (
                backward(g, hidden[g], HB, low) + rim_in[g][tile].astype(F32)
            ).astype(BF16)
            bwd[g][high] = (
                backward(g, hidden[g], HB, high) + rim_in[g][HB + tile].astype(F32)
            ).astype(BF16)
            return carry

        lax.fori_loop(0, HB, bwd_rim, 0, unroll=HB)
        extras_b(g, bwd[g], 0)
        rims(g, rim_out2[g])
        rim2[g][0].start()
        rim2[g][1].start()

    def mixed(g, first, received):
        columns_of_tiles = []
        for tile in range(PAIR):
            at = first + tile
            two = backward(g, bwd[g], 0, at)
            if received is not None:
                two = two + rim_in2[g][received + tile].astype(F32)
            columns_of_tiles.append(
                jnp.concatenate(
                    [
                        hidden[g][HB + at],
                        fwd[g][HB + at],
                        forward(g, fwd[g], at).astype(BF16),
                        bwd[g][at],
                        two.astype(BF16),
                    ],
                    axis=0,
                )
            )
        blocks = jnp.concatenate(columns_of_tiles, axis=1)
        rows_here = pl.ds(g * ROWS, ROWS)
        where = pl.ds(pl.multiple_of(first * T, PAIR * T), PAIR * T)
        total = nn(mix_w[...], blocks) + cur[rows_here, where].astype(F32) + bias_mix
        out[rows_here, where] = total.astype(BF16)

    def store(g, first, count, index):
        where = (pl.ds(g * ROWS, ROWS), pl.ds(first * T, count * T))
        return pltpu.make_async_copy(out.at[where], out_ref.at[where], out_sem.at[3 * g + index])

    stores = []

    def mix_inner(g):
        edge[g][0].wait()
        edge[g][1].wait()
        extras_f(g, fwd[g])

        def step(index, carry):
            mixed(g, HB + index * PAIR, None)
            return carry

        count = (RT - 2 * HB) // PAIR
        lax.fori_loop(0, count, step, 0, unroll=MIXED)
        stores.append(store(g, HB, RT - 2 * HB, 0))
        stores[-1].start()

    def mix_rim(g):
        rim2[g][0].wait()
        rim2[g][1].wait()

        def step(index, carry):
            mixed(g, index * PAIR, index * PAIR)
            mixed(g, RT - HB + index * PAIR, HB + index * PAIR)
            return carry

        lax.fori_loop(0, HB // PAIR, step, 0, unroll=HB // PAIR)
        for first, index in ((0, 1), (RT - HB, 2)):
            stores.append(store(g, first, HB, index))
            stores[-1].start()

    outer_gates(0)

    lane = iota((1, T), 1)
    pad = jnp.zeros((1, T - SLOTS), I32)
    rows = jnp.concatenate([rows_ref[...], pad], axis=1)
    cols = jnp.concatenate([cols_ref[...], pad], axis=1)
    live = (lane >= RT) & (lane < count_ref[0])
    far = jnp.full((1, T), 2 * T, I32)
    perm_f, take_f, keep_f, last_f = segments(jnp.where(live, rows, far), cols)
    perm_b, take_b, keep_b, last_b = segments(jnp.where(live, cols, far), rows)
    table_v[...] = jnp.concatenate(
        [perm_f, take_f, keep_f, last_f, perm_b, take_b, keep_b, last_b], axis=0
    )
    to_scalars = pltpu.make_async_copy(table_v, table, local_sem.at[9])
    to_scalars.start()
    for g in range(GROUPS):
        sums_f[g][0] = jnp.zeros((ROWS, T), F32)
        sums_b[g][0] = jnp.zeros((ROWS, T), F32)

    loads[8].wait()

    def turn(slot, carry):
        tiles_t[slot] = tiles[slot].T
        return carry

    lax.fori_loop(0, SLOTS, turn, 0, unroll=16)
    to_scalars.wait()

    inner_gates(0)
    hop_one(0)
    if GROUPS == 2:
        outer_gates(1)
        backward_two(0)
        inner_gates(1)
        hop_one(1)
        mix_inner(0)
        backward_two(1)
        mix_rim(0)
        mix_inner(1)
        mix_rim(1)
    else:
        backward_two(0)
        mix_inner(0)
        mix_rim(0)

    for group in range(GROUPS):
        for chunk in range(CHUNKS):
            shift(group, chunk).wait_send()
    for copy in stores:
        copy.wait()


def body(
    signal,
    time_weight,
    time_bias,
    mix_weight,
    mix_bias,
    tile_values,
    tile_rows,
    tile_cols,
    tile_count,
):
    width = signal.shape[2]
    whole = DAYS * CH
    hbm = pl.BlockSpec(memory_space=pltpu.HBM)
    panel = pltpu.VMEM((whole, width), BF16)

    def each(*shape):
        return [pltpu.VMEM(*shape) for _ in range(GROUPS)]

    result = pl.pallas_call(
        kernel,
        out_shape=jax.ShapeDtypeStruct((whole, width), BF16),
        in_specs=[hbm] * 9,
        out_specs=pl.BlockSpec(memory_space=pl.ANY),
        scratch_shapes=[
            panel,
            panel,
            pltpu.VMEM((SLOTS, T, T), BF16),
            pltpu.VMEM((SLOTS, T, T), BF16),
            each((RT + 2 * HB, ROWS, T), BF16),
            each((RT + 2 * HB, ROWS, T), BF16),
            each((RT, ROWS, T), BF16),
            each((EXTRA + 1, ROWS, T), F32),
            each((EXTRA + 1, ROWS, T), F32),
            each((2 * HB, ROWS, T), BF16),
            each((2 * HB, ROWS, T), BF16),
            each((2 * HB, ROWS, T), BF16),
            each((2 * HB, ROWS, T), BF16),
            panel,
            pltpu.VMEM((2 * ROWS, 2 * ROWS), BF16),
            pltpu.VMEM((ROWS, 5 * ROWS), BF16),
            pltpu.VMEM((2, CH, 2 * CH), BF16),
            pltpu.VMEM((2 * CH,), F32),
            pltpu.VMEM((CH, 5 * CH), BF16),
            pltpu.VMEM((CH,), F32),
            pltpu.VMEM((1, SLOTS), I32),
            pltpu.VMEM((1, SLOTS), I32),
            pltpu.SMEM((1,), I32),
            pltpu.VMEM((8, T), I32),
            pltpu.SMEM((8, T), I32),
            pltpu.SemaphoreType.DMA((10,)),
            pltpu.SemaphoreType.DMA((GROUPS * CHUNKS,)),
            pltpu.SemaphoreType.DMA((GROUPS * CHUNKS,)),
            pltpu.SemaphoreType.DMA((8 * GROUPS,)),
            pltpu.SemaphoreType.DMA((8 * GROUPS,)),
            pltpu.SemaphoreType.DMA((3 * GROUPS,)),
        ],
        compiler_params=pltpu.CompilerParams(
            collective_id=0, has_side_effects=True, vmem_limit_bytes=56 * 2**20
        ),
    )(
        signal.reshape(whole, width),
        jnp.transpose(time_weight, (0, 2, 1)),
        time_bias,
        mix_weight,
        mix_bias,
        tile_values[0],
        tile_rows,
        tile_cols,
        tile_count,
    )
    return result.reshape(signal.shape)


def solution(mesh):
    placed = (
        P("tm", None, "region"),
        P(),
        P(),
        P(),
        P(),
        P("region", None, None, None),
        P("region", None),
        P("region", None),
        P("region"),
    )
    return jax.shard_map(
        body, mesh=mesh, in_specs=placed, out_specs=P("tm", None, "region"), check_vma=False
    )
```

```python
import jax
import jax.numpy as jnp
from jax import lax
from jax.experimental import pallas as pl
from jax.experimental.pallas import tpu as pltpu
from jax.sharding import PartitionSpec as P

HB = 4
DAYS = 4
CH = 32
T = 128
GROUPS = 1
ROWS = DAYS * CH // GROUPS
SLOTS = 96
RT = 32
EXTRA = SLOTS - RT
CHUNK = 4
PAIR = 2
UNROLL = 64
INNER = 12
MIXED = 4
CHUNKS = RT // CHUNK
MESH = pl.DeviceIdType.MESH
F32 = jnp.float32
BF16 = jnp.bfloat16
I32 = jnp.int32


def iota(shape, dim):
    return lax.broadcasted_iota(I32, shape, dim)


def nn(a, b):
    return jnp.dot(a, b, preferred_element_type=F32)


def segments(keys, takes):
    square = (T, T)
    slot_row = iota(square, 0)
    slot_col = iota(square, 1)
    by_col = jnp.broadcast_to(keys, square)
    by_row = by_col.T
    take_row = jnp.broadcast_to(takes, square).T
    earlier_same = ((by_col == by_row) & (slot_col < slot_row)).astype(I32)
    lower = (by_col < by_row).astype(I32)
    rank = jnp.sum(earlier_same + lower, axis=1, keepdims=True)
    keep = (jnp.sum(earlier_same, axis=1, keepdims=True) > 0).astype(I32)
    at = rank == slot_col
    zero = jnp.zeros(square, I32)
    perm = jnp.sum(jnp.where(at, jnp.minimum(slot_row, SLOTS - 1), zero), axis=0, keepdims=True)
    take = jnp.sum(jnp.where(at, take_row, zero), axis=0, keepdims=True)
    kept = jnp.sum(jnp.where(at, jnp.broadcast_to(keep, square), zero), axis=0, keepdims=True)
    upto = jnp.sum((by_row <= slot_col).astype(I32), axis=0, keepdims=True)
    count = jnp.sum((by_row == slot_col).astype(I32), axis=0, keepdims=True)
    last = jnp.where(count > 0, upto, 0)
    return perm, take, kept, last


def kernel(
    signal_ref,
    time_weight_hbm,
    time_bias_hbm,
    mix_weight_hbm,
    mix_bias_hbm,
    tiles_hbm,
    rows_hbm,
    cols_hbm,
    count_hbm,
    out_ref,
    cur,
    lag,
    tiles,
    tiles_t,
    hidden,
    fwd,
    bwd,
    sums_f,
    sums_b,
    rim_out,
    rim_in,
    rim_out2,
    rim_in2,
    out,
    conv_w,
    mix_w,
    time_weight_ref,
    time_bias_ref,
    mix_weight_ref,
    mix_bias_ref,
    rows_ref,
    cols_ref,
    count_ref,
    table_v,
    table,
    local_sem,
    x_send,
    x_recv,
    r_send,
    r_recv,
    out_sem,
):
    region = lax.axis_index("region")
    tm = lax.axis_index("tm")
    regions = lax.axis_size("region")
    tms = lax.axis_size("tm")
    above, below = (region + 1, tm), (region - 1, tm)
    later, earlier = (region, tm + 1), (region, tm - 1)
    has_above, has_below = region < regions - 1, region > 0
    has_later, has_earlier = tm < tms - 1, tm > 0

    barrier = pltpu.get_barrier_semaphore()
    for there, peer in (
        (has_later, later),
        (has_earlier, earlier),
        (has_above, above),
        (has_below, below),
    ):

        @pl.when(there)
        def _(peer=peer):
            pl.semaphore_signal(barrier, inc=1, device_id=peer, device_id_type=MESH)

    loads = [
        pltpu.make_async_copy(src, dst, local_sem.at[index])
        for index, (src, dst) in enumerate(
            [
                (count_hbm, count_ref),
                (rows_hbm, rows_ref),
                (cols_hbm, cols_ref),
                (time_weight_hbm, time_weight_ref),
                (time_bias_hbm, time_bias_ref),
                (mix_weight_hbm, mix_weight_ref),
                (mix_bias_hbm, mix_bias_ref),
                (signal_ref, cur),
                (tiles_hbm, tiles),
            ]
        )
    ]
    for load in loads:
        load.start()
    peers = sum(
        there.astype(I32) for there in (has_later, has_earlier, has_above, has_below)
    )
    pl.semaphore_wait(barrier, peers)

    def columns(chunk):
        return pl.ds(chunk * (CHUNK * T), CHUNK * T)

    def shift(group, chunk):
        where = (pl.ds(group * ROWS, ROWS), columns(chunk))
        index = group * CHUNKS + chunk
        return pltpu.make_async_remote_copy(
            src_ref=signal_ref.at[where],
            dst_ref=lag.at[where],
            send_sem=x_send.at[index],
            recv_sem=x_recv.at[index],
            device_id=later,
            device_id_type=MESH,
        )

    order = [0, CHUNKS - 1] + list(range(1, CHUNKS - 1))

    @pl.when(has_later)
    def _():
        for group in range(GROUPS):
            for chunk in order:
                shift(group, chunk).start()

    @pl.when(jnp.logical_not(has_earlier))
    def _():
        lag[...] = jnp.zeros(lag.shape, BF16)

    @pl.when(jnp.logical_not(has_below))
    def _():
        for g in range(GROUPS):
            for ref, first in ((hidden[g], 0), (fwd[g], 0), (rim_in[g], 0), (rim_in2[g], 0)):
                ref[first : first + HB] = jnp.zeros((HB, ROWS, T), BF16)

    @pl.when(jnp.logical_not(has_above))
    def _():
        for g in range(GROUPS):
            for ref, first in (
                (hidden[g], HB + RT),
                (fwd[g], HB + RT),
                (rim_in[g], HB),
                (rim_in2[g], HB),
            ):
                ref[first : first + HB] = jnp.zeros((HB, ROWS, T), BF16)

    for load in loads[:7]:
        load.wait()

    spread = (lax.rem(iota((ROWS, CH), 0), CH) == iota((ROWS, CH), 1)).astype(BF16)
    same_day = iota((ROWS, ROWS), 0) // CH == iota((ROWS, ROWS), 1) // CH
    for part in range(2):
        tall = [nn(spread, time_weight_ref[tap]).astype(BF16) for tap in range(2)]
        pick = (
            iota((2 * CH, ROWS), 0) == part * CH + lax.rem(iota((2 * CH, ROWS), 1), CH)
        ).astype(BF16)
        for tap in range(2):
            wide = nn(tall[tap], pick).T * (1.0 if part == 0 else 0.5)
            conv_w[part * ROWS : (part + 1) * ROWS, tap * ROWS : (tap + 1) * ROWS] = jnp.where(
                same_day, wide, 0.0
            ).astype(BF16)
    tall_mix = nn(spread, mix_weight_ref[...]).astype(BF16)
    for branch in range(5):
        pick = (
            iota((5 * CH, ROWS), 0) == branch * CH + lax.rem(iota((5 * CH, ROWS), 1), CH)
        ).astype(BF16)
        mix_w[:, branch * ROWS : (branch + 1) * ROWS] = jnp.where(
            same_day, nn(tall_mix, pick), 0.0
        ).astype(BF16)
    channel = lax.rem(iota((ROWS, 1), 0), CH)

    def column_of(values, first):
        width = values.shape[1]
        hit = iota((ROWS, width), 1) == channel + first
        return jnp.sum(jnp.where(hit, jnp.broadcast_to(values, (ROWS, width)), 0.0), 1, keepdims=True)

    time_bias = time_bias_ref[...].reshape(1, 2 * CH)
    bias_filter = column_of(time_bias, 0)
    bias_gate = column_of(time_bias, CH) * 0.5
    bias_mix = column_of(mix_bias_ref[...].reshape(1, CH), 0)
    loads[7].wait()

    def to_region(src, dst, index, peer):
        return pltpu.make_async_remote_copy(
            src_ref=src,
            dst_ref=dst,
            send_sem=r_send.at[index],
            recv_sem=r_recv.at[index],
            device_id=peer,
            device_id_type=MESH,
        )

    def start_low(pair):
        pl.when(has_below)(pair[0].start)

    def start_high(pair):
        pl.when(has_above)(pair[1].start)

    def receive(pair):
        pl.when(has_above)(pair[0].wait_recv)
        pl.when(has_below)(pair[1].wait_recv)

    def sent(pair):
        pl.when(has_below)(pair[0].wait_send)
        pl.when(has_above)(pair[1].wait_send)

    first_tiles, last_tiles = pl.ds(HB, HB), pl.ds(RT, HB)
    from_below, from_above = pl.ds(0, HB), pl.ds(HB + RT, HB)
    rim_first, rim_last = pl.ds(0, HB), pl.ds(HB, HB)
    halo, rim, edge, rim2 = [], [], [], []
    for g in range(GROUPS):
        base = 8 * g
        halo.append(
            (
                to_region(hidden[g].at[first_tiles], hidden[g].at[from_above], base, below),
                to_region(hidden[g].at[last_tiles], hidden[g].at[from_below], base + 1, above),
            )
        )
        rim.append(
            (
                to_region(rim_out[g].at[rim_first], rim_in[g].at[rim_last], base + 2, below),
                to_region(rim_out[g].at[rim_last], rim_in[g].at[rim_first], base + 3, above),
            )
        )
        edge.append(
            (
                to_region(fwd[g].at[first_tiles], fwd[g].at[from_above], base + 4, below),
                to_region(fwd[g].at[last_tiles], fwd[g].at[from_below], base + 5, above),
            )
        )
        rim2.append(
            (
                to_region(rim_out2[g].at[rim_first], rim_in2[g].at[rim_last], base + 6, below),
                to_region(rim_out2[g].at[rim_last], rim_in2[g].at[rim_first], base + 7, above),
            )
        )

    def gate(group, chunk):
        @pl.when(has_earlier)
        def _():
            shift(group, chunk).wait_recv()

        rows_here = pl.ds(group * ROWS, ROWS)

        def part(index, carry):
            first = chunk * CHUNK + index * PAIR
            where = pl.ds(pl.multiple_of(first * T, PAIR * T), PAIR * T)
            days = jnp.concatenate([lag[rows_here, where], cur[rows_here, where]], axis=0)
            pre = nn(conv_w[...], days)
            value = jnp.tanh(pre[:ROWS] + bias_filter) * (
                0.5 + 0.5 * jnp.tanh(pre[ROWS:] + bias_gate)
            )
            value = value.astype(BF16)
            for tile in range(PAIR):
                hidden[group][HB + first + tile] = value[:, tile * T : (tile + 1) * T]
            return carry

        lax.fori_loop(0, CHUNK // PAIR, part, 0, unroll=CHUNK // PAIR)

    def outer_gates(group):
        gate(group, 0)
        start_low(halo[group])
        gate(group, CHUNKS - 1)
        start_high(halo[group])

    def inner_gates(group):
        for chunk in range(1, CHUNKS - 1):
            gate(group, chunk)

    def extras(source, base, values, sums, first):
        def add(place, running):
            product = nn(source[table[first + 1, place] + base], values[table[first, place]])
            running = jnp.where(table[first + 2, place] > 0, running, 0.0) + product
            sums[place + 1] = running
            return running

        lax.fori_loop(0, EXTRA, add, jnp.zeros((ROWS, T), F32), unroll=UNROLL)

    def extras_f(g, source):
        extras(source, 0, tiles_t, sums_f[g], 0)

    def extras_b(g, source, base):
        extras(source, base, tiles, sums_b[g], 4)

    def rims(g, target):
        def fill(tile, carry):
            target[tile] = sums_b[g][table[7, tile]].astype(BF16)
            target[HB + tile] = sums_b[g][table[7, HB + RT + tile]].astype(BF16)
            return carry

        lax.fori_loop(0, HB, fill, 0, unroll=HB)

    def forward(g, source, tile):
        return nn(source[HB + tile], tiles_t[tile]) + sums_f[g][table[3, tile]]

    def backward(g, source, base, tile):
        return nn(source[base + tile], tiles[tile]) + sums_b[g][table[7, HB + tile]]

    def hop_one(g):
        receive(halo[g])
        extras_b(g, hidden[g], HB)
        rims(g, rim_out[g])
        start_low(rim[g])
        start_high(rim[g])
        extras_f(g, hidden[g])

        def fwd_tile(tile, carry):
            fwd[g][HB + tile] = forward(g, hidden[g], tile).astype(BF16)
            return carry

        def fwd_rim(tile, carry):
            return fwd_tile(RT - HB + tile, fwd_tile(tile, carry))

        lax.fori_loop(0, HB, fwd_rim, 0, unroll=HB)
        start_low(edge[g])
        start_high(edge[g])

        def inner(tile, carry):
            bwd[g][tile] = backward(g, hidden[g], HB, tile).astype(BF16)
            return fwd_tile(tile, carry)

        lax.fori_loop(HB, RT - HB, inner, 0, unroll=INNER)

    def backward_two(g):
        receive(rim[g])

        def bwd_rim(tile, carry):
            low, high = tile, RT - HB + tile
            bwd[g][low] = (
                backward(g, hidden[g], HB, low) + rim_in[g][tile].astype(F32)
            ).astype(BF16)
            bwd[g][high] = (
                backward(g, hidden[g], HB, high) + rim_in[g][HB + tile].astype(F32)
            ).astype(BF16)
            return carry

        lax.fori_loop(0, HB, bwd_rim, 0, unroll=HB)
        extras_b(g, bwd[g], 0)
        rims(g, rim_out2[g])
        start_low(rim2[g])
        start_high(rim2[g])

    def mixed(g, first, received):
        columns_of_tiles = []
        for tile in range(PAIR):
            at = first + tile
            two = backward(g, bwd[g], 0, at)
            if received is not None:
                two = two + rim_in2[g][received + tile].astype(F32)
            columns_of_tiles.append(
                jnp.concatenate(
                    [
                        hidden[g][HB + at],
                        fwd[g][HB + at],
                        forward(g, fwd[g], at).astype(BF16),
                        bwd[g][at],
                        two.astype(BF16),
                    ],
                    axis=0,
                )
            )
        blocks = jnp.concatenate(columns_of_tiles, axis=1)
        rows_here = pl.ds(g * ROWS, ROWS)
        where = pl.ds(pl.multiple_of(first * T, PAIR * T), PAIR * T)
        total = nn(mix_w[...], blocks) + cur[rows_here, where].astype(F32) + bias_mix
        out[rows_here, where] = total.astype(BF16)

    def store(g, first, count, index):
        where = (pl.ds(g * ROWS, ROWS), pl.ds(first * T, count * T))
        return pltpu.make_async_copy(out.at[where], out_ref.at[where], out_sem.at[3 * g + index])

    stores = []

    def mix_inner(g):
        receive(edge[g])
        extras_f(g, fwd[g])

        def step(index, carry):
            mixed(g, HB + index * PAIR, None)
            return carry

        count = (RT - 2 * HB) // PAIR
        lax.fori_loop(0, count, step, 0, unroll=MIXED)
        stores.append(store(g, HB, RT - 2 * HB, 0))
        stores[-1].start()

    def mix_rim(g):
        receive(rim2[g])

        def step(index, carry):
            mixed(g, index * PAIR, index * PAIR)
            mixed(g, RT - HB + index * PAIR, HB + index * PAIR)
            return carry

        lax.fori_loop(0, HB // PAIR, step, 0, unroll=HB // PAIR)
        for first, index in ((0, 1), (RT - HB, 2)):
            stores.append(store(g, first, HB, index))
            stores[-1].start()

    outer_gates(0)

    lane = iota((1, T), 1)
    pad = jnp.zeros((1, T - SLOTS), I32)
    rows = jnp.concatenate([rows_ref[...], pad], axis=1)
    cols = jnp.concatenate([cols_ref[...], pad], axis=1)
    live = (lane >= RT) & (lane < count_ref[0])
    far = jnp.full((1, T), 2 * T, I32)
    perm_f, take_f, keep_f, last_f = segments(jnp.where(live, rows, far), cols)
    perm_b, take_b, keep_b, last_b = segments(jnp.where(live, cols, far), rows)
    table_v[...] = jnp.concatenate(
        [perm_f, take_f, keep_f, last_f, perm_b, take_b, keep_b, last_b], axis=0
    )
    to_scalars = pltpu.make_async_copy(table_v, table, local_sem.at[9])
    to_scalars.start()
    for g in range(GROUPS):
        sums_f[g][0] = jnp.zeros((ROWS, T), F32)
        sums_b[g][0] = jnp.zeros((ROWS, T), F32)

    loads[8].wait()

    def turn(slot, carry):
        tiles_t[slot] = tiles[slot].T
        return carry

    lax.fori_loop(0, SLOTS, turn, 0, unroll=16)
    to_scalars.wait()

    inner_gates(0)
    hop_one(0)
    backward_two(0)
    mix_inner(0)
    mix_rim(0)

    @pl.when(has_later)
    def _():
        for group in range(GROUPS):
            for chunk in range(CHUNKS):
                shift(group, chunk).wait_send()

    for group in range(GROUPS):
        for pair in (halo[group], rim[group], edge[group], rim2[group]):
            sent(pair)
    for copy in stores:
        copy.wait()


def body(
    signal,
    time_weight,
    time_bias,
    mix_weight,
    mix_bias,
    tile_values,
    tile_rows,
    tile_cols,
    tile_count,
):
    width = signal.shape[2]
    whole = DAYS * CH
    hbm = pl.BlockSpec(memory_space=pltpu.HBM)
    panel = pltpu.VMEM((whole, width), BF16)

    def each(*shape):
        return [pltpu.VMEM(*shape) for _ in range(GROUPS)]

    result = pl.pallas_call(
        kernel,
        out_shape=jax.ShapeDtypeStruct((whole, width), BF16),
        in_specs=[hbm] * 9,
        out_specs=pl.BlockSpec(memory_space=pl.ANY),
        scratch_shapes=[
            panel,
            panel,
            pltpu.VMEM((SLOTS, T, T), BF16),
            pltpu.VMEM((SLOTS, T, T), BF16),
            each((RT + 2 * HB, ROWS, T), BF16),
            each((RT + 2 * HB, ROWS, T), BF16),
            each((RT, ROWS, T), BF16),
            each((EXTRA + 1, ROWS, T), F32),
            each((EXTRA + 1, ROWS, T), F32),
            each((2 * HB, ROWS, T), BF16),
            each((2 * HB, ROWS, T), BF16),
            each((2 * HB, ROWS, T), BF16),
            each((2 * HB, ROWS, T), BF16),
            panel,
            pltpu.VMEM((2 * ROWS, 2 * ROWS), BF16),
            pltpu.VMEM((ROWS, 5 * ROWS), BF16),
            pltpu.VMEM((2, CH, 2 * CH), BF16),
            pltpu.VMEM((2 * CH,), F32),
            pltpu.VMEM((CH, 5 * CH), BF16),
            pltpu.VMEM((CH,), F32),
            pltpu.VMEM((1, SLOTS), I32),
            pltpu.VMEM((1, SLOTS), I32),
            pltpu.SMEM((1,), I32),
            pltpu.VMEM((8, T), I32),
            pltpu.SMEM((8, T), I32),
            pltpu.SemaphoreType.DMA((10,)),
            pltpu.SemaphoreType.DMA((GROUPS * CHUNKS,)),
            pltpu.SemaphoreType.DMA((GROUPS * CHUNKS,)),
            pltpu.SemaphoreType.DMA((8 * GROUPS,)),
            pltpu.SemaphoreType.DMA((8 * GROUPS,)),
            pltpu.SemaphoreType.DMA((3 * GROUPS,)),
        ],
        compiler_params=pltpu.CompilerParams(
            collective_id=0, has_side_effects=True, vmem_limit_bytes=56 * 2**20
        ),
    )(
        signal.reshape(whole, width),
        jnp.transpose(time_weight, (0, 2, 1)),
        time_bias,
        mix_weight,
        mix_bias,
        tile_values[0],
        tile_rows,
        tile_cols,
        tile_count,
    )
    return result.reshape(signal.shape)


def solution(mesh):
    placed = (
        P("tm", None, "region"),
        P(),
        P(),
        P(),
        P(),
        P("region", None, None, None),
        P("region", None),
        P("region", None),
        P("region"),
    )
    return jax.shard_map(
        body, mesh=mesh, in_specs=placed, out_specs=P("tm", None, "region"), check_vma=False
    )
```

```python
import jax
import jax.numpy as jnp
from jax import lax
from jax.experimental import pallas as pl
from jax.experimental.pallas import tpu as pltpu
from jax.sharding import PartitionSpec as P

HB = 4
DAYS = 4
CH = 32
T = 128
GROUPS = 1
ROWS = DAYS * CH // GROUPS
SLOTS = 96
RT = 32
EXTRA = SLOTS - RT
CHUNK = 4
PAIR = 2
HALVES = 2
HALF = ROWS // HALVES
UNROLL = 64
INNER = 12
MIXED = 4
CHUNKS = RT // CHUNK
MESH = pl.DeviceIdType.MESH
F32 = jnp.float32
BF16 = jnp.bfloat16
I32 = jnp.int32


def iota(shape, dim):
    return lax.broadcasted_iota(I32, shape, dim)


def nn(a, b):
    return jnp.dot(a, b, preferred_element_type=F32)


def segments(keys, takes):
    square = (T, T)
    slot_row = iota(square, 0)
    slot_col = iota(square, 1)
    by_col = jnp.broadcast_to(keys, square)
    by_row = by_col.T
    take_row = jnp.broadcast_to(takes, square).T
    earlier_same = ((by_col == by_row) & (slot_col < slot_row)).astype(I32)
    lower = (by_col < by_row).astype(I32)
    rank = jnp.sum(earlier_same + lower, axis=1, keepdims=True)
    keep = (jnp.sum(earlier_same, axis=1, keepdims=True) > 0).astype(I32)
    at = rank == slot_col
    zero = jnp.zeros(square, I32)
    perm = jnp.sum(jnp.where(at, jnp.minimum(slot_row, SLOTS - 1), zero), axis=0, keepdims=True)
    take = jnp.sum(jnp.where(at, take_row, zero), axis=0, keepdims=True)
    kept = jnp.sum(jnp.where(at, jnp.broadcast_to(keep, square), zero), axis=0, keepdims=True)
    upto = jnp.sum((by_row <= slot_col).astype(I32), axis=0, keepdims=True)
    count = jnp.sum((by_row == slot_col).astype(I32), axis=0, keepdims=True)
    last = jnp.where(count > 0, upto, 0)
    return perm, take, kept, last


def kernel(
    signal_ref,
    time_weight_hbm,
    time_bias_hbm,
    mix_weight_hbm,
    mix_bias_hbm,
    tiles_hbm,
    rows_hbm,
    cols_hbm,
    count_hbm,
    out_ref,
    cur,
    lag,
    tiles,
    tiles_t,
    hidden,
    fwd,
    bwd,
    sums_f,
    sums_b,
    rim_out,
    rim_in,
    rim_out2,
    rim_in2,
    out,
    conv_w,
    mix_w,
    time_weight_ref,
    time_bias_ref,
    mix_weight_ref,
    mix_bias_ref,
    rows_ref,
    cols_ref,
    count_ref,
    table_v,
    table,
    local_sem,
    x_send,
    x_recv,
    r_send,
    r_recv,
    out_sem,
):
    region = lax.axis_index("region")
    tm = lax.axis_index("tm")
    regions = lax.axis_size("region")
    tms = lax.axis_size("tm")
    above, below = (region + 1, tm), (region - 1, tm)
    later, earlier = (region, tm + 1), (region, tm - 1)
    has_above, has_below = region < regions - 1, region > 0
    has_later, has_earlier = tm < tms - 1, tm > 0

    barrier = pltpu.get_barrier_semaphore()
    for there, peer in (
        (has_later, later),
        (has_earlier, earlier),
        (has_above, above),
        (has_below, below),
    ):

        @pl.when(there)
        def _(peer=peer):
            pl.semaphore_signal(barrier, inc=1, device_id=peer, device_id_type=MESH)

    loads = [
        pltpu.make_async_copy(src, dst, local_sem.at[index])
        for index, (src, dst) in enumerate(
            [
                (count_hbm, count_ref),
                (rows_hbm, rows_ref),
                (cols_hbm, cols_ref),
                (time_weight_hbm, time_weight_ref),
                (time_bias_hbm, time_bias_ref),
                (mix_weight_hbm, mix_weight_ref),
                (mix_bias_hbm, mix_bias_ref),
                (signal_ref, cur),
                (tiles_hbm, tiles),
            ]
        )
    ]
    for load in loads[:7]:
        load.start()
    peers = sum(
        there.astype(I32) for there in (has_later, has_earlier, has_above, has_below)
    )
    pl.semaphore_wait(barrier, peers)

    def columns(chunk):
        return pl.ds(chunk * (CHUNK * T), CHUNK * T)

    def shift(group, chunk):
        where = (pl.ds(group * ROWS, ROWS), columns(chunk))
        index = group * CHUNKS + chunk
        return pltpu.make_async_remote_copy(
            src_ref=signal_ref.at[where],
            dst_ref=lag.at[where],
            send_sem=x_send.at[index],
            recv_sem=x_recv.at[index],
            device_id=later,
            device_id_type=MESH,
        )

    order = [0, CHUNKS - 1] + list(range(1, CHUNKS - 1))

    @pl.when(has_later)
    def _():
        for group in range(GROUPS):
            for chunk in order:
                shift(group, chunk).start()

    @pl.when(jnp.logical_not(has_earlier))
    def _():
        lag[...] = jnp.zeros(lag.shape, BF16)

    @pl.when(jnp.logical_not(has_below))
    def _():
        for g in range(GROUPS):
            for ref, first in ((hidden[g], 0), (fwd[g], 0), (rim_in[g], 0), (rim_in2[g], 0)):
                ref[first : first + HB] = jnp.zeros((HB, ROWS, T), BF16)

    @pl.when(jnp.logical_not(has_above))
    def _():
        for g in range(GROUPS):
            for ref, first in (
                (hidden[g], HB + RT),
                (fwd[g], HB + RT),
                (rim_in[g], HB),
                (rim_in2[g], HB),
            ):
                ref[first : first + HB] = jnp.zeros((HB, ROWS, T), BF16)

    for load in loads[7:]:
        load.start()
    for load in loads[:7]:
        load.wait()

    spread = (lax.rem(iota((ROWS, CH), 0), CH) == iota((ROWS, CH), 1)).astype(BF16)
    same_day = iota((ROWS, ROWS), 0) // CH == iota((ROWS, ROWS), 1) // CH
    for part in range(2):
        tall = [nn(spread, time_weight_ref[tap]).astype(BF16) for tap in range(2)]
        pick = (
            iota((2 * CH, ROWS), 0) == part * CH + lax.rem(iota((2 * CH, ROWS), 1), CH)
        ).astype(BF16)
        for tap in range(2):
            wide = nn(tall[tap], pick).T * (1.0 if part == 0 else 0.5)
            conv_w[part * ROWS : (part + 1) * ROWS, tap * ROWS : (tap + 1) * ROWS] = jnp.where(
                same_day, wide, 0.0
            ).astype(BF16)
    tall_mix = nn(spread, mix_weight_ref[...]).astype(BF16)
    for branch in range(5):
        pick = (
            iota((5 * CH, ROWS), 0) == branch * CH + lax.rem(iota((5 * CH, ROWS), 1), CH)
        ).astype(BF16)
        mix_w[:, branch * ROWS : (branch + 1) * ROWS] = jnp.where(
            same_day, nn(tall_mix, pick), 0.0
        ).astype(BF16)
    channel = lax.rem(iota((ROWS, 1), 0), CH)

    def column_of(values, first):
        width = values.shape[1]
        hit = iota((ROWS, width), 1) == channel + first
        return jnp.sum(jnp.where(hit, jnp.broadcast_to(values, (ROWS, width)), 0.0), 1, keepdims=True)

    time_bias = time_bias_ref[...].reshape(1, 2 * CH)
    bias_filter = column_of(time_bias, 0)
    bias_gate = column_of(time_bias, CH) * 0.5
    bias_mix = column_of(mix_bias_ref[...].reshape(1, CH), 0)
    loads[7].wait()

    def to_region(src, dst, index, peer):
        return pltpu.make_async_remote_copy(
            src_ref=src,
            dst_ref=dst,
            send_sem=r_send.at[index],
            recv_sem=r_recv.at[index],
            device_id=peer,
            device_id_type=MESH,
        )

    def start_low(pair):
        pl.when(has_below)(pair[0].start)

    def start_high(pair):
        pl.when(has_above)(pair[1].start)

    def receive(pair):
        pl.when(has_above)(pair[0].wait_recv)
        pl.when(has_below)(pair[1].wait_recv)

    def sent(pair):
        pl.when(has_below)(pair[0].wait_send)
        pl.when(has_above)(pair[1].wait_send)

    def half_rows(h):
        return pl.ds(h * HALF, HALF)

    first_tiles, last_tiles = pl.ds(HB, HB), pl.ds(RT, HB)
    from_below, from_above = pl.ds(0, HB), pl.ds(HB + RT, HB)
    rim_first, rim_last = pl.ds(0, HB), pl.ds(HB, HB)
    halo, rim, edge, rim2 = [], [], [], []
    for g in range(GROUPS):
        base = 12 * g
        halo.append(
            (
                to_region(hidden[g].at[first_tiles], hidden[g].at[from_above], base, below),
                to_region(hidden[g].at[last_tiles], hidden[g].at[from_below], base + 1, above),
            )
        )
        rim.append(
            [
                (
                    to_region(
                        rim_out[g].at[rim_first, half_rows(h)],
                        rim_in[g].at[rim_last, half_rows(h)],
                        base + 2 + 6 * h,
                        below,
                    ),
                    to_region(
                        rim_out[g].at[rim_last, half_rows(h)],
                        rim_in[g].at[rim_first, half_rows(h)],
                        base + 3 + 6 * h,
                        above,
                    ),
                )
                for h in range(HALVES)
            ]
        )
        edge.append(
            (
                to_region(fwd[g].at[first_tiles], fwd[g].at[from_above], base + 4, below),
                to_region(fwd[g].at[last_tiles], fwd[g].at[from_below], base + 5, above),
            )
        )
        rim2.append(
            [
                (
                    to_region(
                        rim_out2[g].at[rim_first, half_rows(h)],
                        rim_in2[g].at[rim_last, half_rows(h)],
                        base + 6 + 4 * h,
                        below,
                    ),
                    to_region(
                        rim_out2[g].at[rim_last, half_rows(h)],
                        rim_in2[g].at[rim_first, half_rows(h)],
                        base + 7 + 4 * h,
                        above,
                    ),
                )
                for h in range(HALVES)
            ]
        )

    def gate(group, chunk):
        @pl.when(has_earlier)
        def _():
            shift(group, chunk).wait_recv()

        rows_here = pl.ds(group * ROWS, ROWS)

        def part(index, carry):
            first = chunk * CHUNK + index * PAIR
            where = pl.ds(pl.multiple_of(first * T, PAIR * T), PAIR * T)
            days = jnp.concatenate([lag[rows_here, where], cur[rows_here, where]], axis=0)
            pre = nn(conv_w[...], days)
            value = jnp.tanh(pre[:ROWS] + bias_filter) * (
                0.5 + 0.5 * jnp.tanh(pre[ROWS:] + bias_gate)
            )
            value = value.astype(BF16)
            for tile in range(PAIR):
                hidden[group][HB + first + tile] = value[:, tile * T : (tile + 1) * T]
            return carry

        lax.fori_loop(0, CHUNK // PAIR, part, 0, unroll=CHUNK // PAIR)

    def outer_gates(group):
        gate(group, 0)
        start_low(halo[group])
        gate(group, CHUNKS - 1)
        start_high(halo[group])

    def inner_gates(group):
        for chunk in range(1, CHUNKS - 1):
            gate(group, chunk)

    def extras(source, base, values, sums, first, start, count):
        here = pl.ds(start, count)

        def add(place, running):
            product = nn(
                source[table[first + 1, place] + base, here, :], values[table[first, place]]
            )
            running = jnp.where(table[first + 2, place] > 0, running, 0.0) + product
            sums[place + 1, here, :] = running
            return running

        lax.fori_loop(0, EXTRA, add, jnp.zeros((count, T), F32), unroll=UNROLL)

    def extras_f(g, source):
        extras(source, 0, tiles_t, sums_f[g], 0, 0, ROWS)

    def extras_b(g, source, base, h):
        extras(source, base, tiles, sums_b[g], 4, h * HALF, HALF)

    def rims(g, target, h):
        here = half_rows(h)

        def fill(tile, carry):
            target[tile, here, :] = sums_b[g][table[7, tile], here, :].astype(BF16)
            target[HB + tile, here, :] = sums_b[g][table[7, HB + RT + tile], here, :].astype(BF16)
            return carry

        lax.fori_loop(0, HB, fill, 0, unroll=HB)

    def forward(g, source, tile):
        return nn(source[HB + tile], tiles_t[tile]) + sums_f[g][table[3, tile]]

    def backward(g, source, base, tile):
        return nn(source[base + tile], tiles[tile]) + sums_b[g][table[7, HB + tile]]

    def hop_one(g):
        receive(halo[g])
        for h in range(HALVES):
            extras_b(g, hidden[g], HB, h)
            rims(g, rim_out[g], h)
            start_low(rim[g][h])
            start_high(rim[g][h])
        extras_f(g, hidden[g])

        def fwd_tile(tile, carry):
            fwd[g][HB + tile] = forward(g, hidden[g], tile).astype(BF16)
            return carry

        def fwd_rim(tile, carry):
            return fwd_tile(RT - HB + tile, fwd_tile(tile, carry))


        def inner(tile, carry):
            bwd[g][tile] = backward(g, hidden[g], HB, tile).astype(BF16)
            return fwd_tile(tile, carry)

        lax.fori_loop(HB, RT - HB, inner, 0, unroll=INNER)
        lax.fori_loop(0, HB, fwd_rim, 0, unroll=HB)
        start_low(edge[g])
        start_high(edge[g])

    def backward_two(g):
        for h in range(HALVES):
            here = half_rows(h)
            receive(rim[g][h])

            def bwd_rim(tile, carry):
                for at, arrived in ((tile, tile), (RT - HB + tile, HB + tile)):
                    total = nn(hidden[g][HB + at, here, :], tiles[at])
                    total = total + sums_b[g][table[7, HB + at], here, :]
                    total = total + rim_in[g][arrived, here, :].astype(F32)
                    bwd[g][at, here, :] = total.astype(BF16)
                return carry

            lax.fori_loop(0, HB, bwd_rim, 0, unroll=HB)
            extras_b(g, bwd[g], 0, h)
            rims(g, rim_out2[g], h)
            start_low(rim2[g][h])
            start_high(rim2[g][h])

    def mixed(g, first, received):
        columns_of_tiles = []
        for tile in range(PAIR):
            at = first + tile
            two = backward(g, bwd[g], 0, at)
            if received is not None:
                two = two + rim_in2[g][received + tile].astype(F32)
            columns_of_tiles.append(
                jnp.concatenate(
                    [
                        hidden[g][HB + at],
                        fwd[g][HB + at],
                        forward(g, fwd[g], at).astype(BF16),
                        bwd[g][at],
                        two.astype(BF16),
                    ],
                    axis=0,
                )
            )
        blocks = jnp.concatenate(columns_of_tiles, axis=1)
        rows_here = pl.ds(g * ROWS, ROWS)
        where = pl.ds(pl.multiple_of(first * T, PAIR * T), PAIR * T)
        total = nn(mix_w[...], blocks) + cur[rows_here, where].astype(F32) + bias_mix
        out[rows_here, where] = total.astype(BF16)

    def store(g, first, count, index):
        where = (pl.ds(g * ROWS, ROWS), pl.ds(first * T, count * T))
        return pltpu.make_async_copy(out.at[where], out_ref.at[where], out_sem.at[3 * g + index])

    stores = []

    def mix_inner(g):
        receive(edge[g])
        extras_f(g, fwd[g])

        def step(index, carry):
            mixed(g, HB + index * PAIR, None)
            return carry

        count = (RT - 2 * HB) // PAIR
        lax.fori_loop(0, count, step, 0, unroll=MIXED)
        stores.append(store(g, HB, RT - 2 * HB, 0))
        stores[-1].start()

    def mix_rim(g):
        for h in range(HALVES):
            receive(rim2[g][h])

        def step(index, carry):
            mixed(g, index * PAIR, index * PAIR)
            mixed(g, RT - HB + index * PAIR, HB + index * PAIR)
            return carry

        lax.fori_loop(0, HB // PAIR, step, 0, unroll=HB // PAIR)
        for first, index in ((0, 1), (RT - HB, 2)):
            stores.append(store(g, first, HB, index))
            stores[-1].start()

    outer_gates(0)

    lane = iota((1, T), 1)
    pad = jnp.zeros((1, T - SLOTS), I32)
    rows = jnp.concatenate([rows_ref[...], pad], axis=1)
    cols = jnp.concatenate([cols_ref[...], pad], axis=1)
    live = (lane >= RT) & (lane < count_ref[...])
    far = jnp.full((1, T), 2 * T, I32)
    perm_f, take_f, keep_f, last_f = segments(jnp.where(live, rows, far), cols)
    perm_b, take_b, keep_b, last_b = segments(jnp.where(live, cols, far), rows)
    table_v[...] = jnp.concatenate(
        [perm_f, take_f, keep_f, last_f, perm_b, take_b, keep_b, last_b], axis=0
    )
    to_scalars = pltpu.make_async_copy(table_v, table, local_sem.at[9])
    to_scalars.start()
    for g in range(GROUPS):
        sums_f[g][0] = jnp.zeros((ROWS, T), F32)
        sums_b[g][0] = jnp.zeros((ROWS, T), F32)

    loads[8].wait()

    def turn(slot, carry):
        tiles_t[slot] = tiles[slot].T
        return carry

    lax.fori_loop(0, SLOTS, turn, 0, unroll=16)
    to_scalars.wait()

    inner_gates(0)
    hop_one(0)
    backward_two(0)
    mix_inner(0)
    mix_rim(0)

    @pl.when(has_later)
    def _():
        for group in range(GROUPS):
            for chunk in range(CHUNKS):
                shift(group, chunk).wait_send()

    for group in range(GROUPS):
        for pair in (halo[group], edge[group], *rim[group], *rim2[group]):
            sent(pair)
    for copy in stores:
        copy.wait()


def body(
    signal,
    time_weight,
    time_bias,
    mix_weight,
    mix_bias,
    tile_values,
    tile_rows,
    tile_cols,
    tile_count,
):
    width = signal.shape[2]
    whole = DAYS * CH
    hbm = pl.BlockSpec(memory_space=pltpu.HBM)
    panel = pltpu.VMEM((whole, width), BF16)

    def each(*shape):
        return [pltpu.VMEM(*shape) for _ in range(GROUPS)]

    result = pl.pallas_call(
        kernel,
        out_shape=jax.ShapeDtypeStruct((whole, width), BF16),
        in_specs=[hbm] * 9,
        out_specs=pl.BlockSpec(memory_space=pl.ANY),
        scratch_shapes=[
            panel,
            panel,
            pltpu.VMEM((SLOTS, T, T), BF16),
            pltpu.VMEM((SLOTS, T, T), BF16),
            each((RT + 2 * HB, ROWS, T), BF16),
            each((RT + 2 * HB, ROWS, T), BF16),
            each((RT, ROWS, T), BF16),
            each((EXTRA + 1, ROWS, T), F32),
            each((EXTRA + 1, ROWS, T), F32),
            each((2 * HB, ROWS, T), BF16),
            each((2 * HB, ROWS, T), BF16),
            each((2 * HB, ROWS, T), BF16),
            each((2 * HB, ROWS, T), BF16),
            panel,
            pltpu.VMEM((2 * ROWS, 2 * ROWS), BF16),
            pltpu.VMEM((ROWS, 5 * ROWS), BF16),
            pltpu.VMEM((2, CH, 2 * CH), BF16),
            pltpu.VMEM((2 * CH,), F32),
            pltpu.VMEM((CH, 5 * CH), BF16),
            pltpu.VMEM((CH,), F32),
            pltpu.VMEM((1, SLOTS), I32),
            pltpu.VMEM((1, SLOTS), I32),
            pltpu.VMEM((1, 1), I32),
            pltpu.VMEM((8, T), I32),
            pltpu.SMEM((8, T), I32),
            pltpu.SemaphoreType.DMA((10,)),
            pltpu.SemaphoreType.DMA((GROUPS * CHUNKS,)),
            pltpu.SemaphoreType.DMA((GROUPS * CHUNKS,)),
            pltpu.SemaphoreType.DMA((12 * GROUPS,)),
            pltpu.SemaphoreType.DMA((12 * GROUPS,)),
            pltpu.SemaphoreType.DMA((3 * GROUPS,)),
        ],
        compiler_params=pltpu.CompilerParams(
            collective_id=0, has_side_effects=True, vmem_limit_bytes=56 * 2**20
        ),
    )(
        signal.reshape(whole, width),
        jnp.transpose(time_weight, (0, 2, 1)),
        time_bias,
        mix_weight,
        mix_bias,
        tile_values[0],
        tile_rows,
        tile_cols,
        tile_count.reshape(1, 1),
    )
    return result.reshape(signal.shape)


def solution(mesh):
    placed = (
        P("tm", None, "region"),
        P(),
        P(),
        P(),
        P(),
        P("region", None, None, None),
        P("region", None),
        P("region", None),
        P("region"),
    )
    return jax.shard_map(
        body, mesh=mesh, in_specs=placed, out_specs=P("tm", None, "region"), check_vma=False
    )
```

```python
import jax
import jax.numpy as jnp
from jax import lax
from jax.experimental import pallas as pl
from jax.experimental.pallas import tpu as pltpu
from jax.sharding import PartitionSpec as P

HB = 4
DAYS = 4
CH = 32
T = 128
GROUPS = 1
ROWS = DAYS * CH // GROUPS
SLOTS = 96
RT = 32
EXTRA = SLOTS - RT
CHUNK = 4
PAIR = 2
HALVES = 2
HALF = ROWS // HALVES
UNROLL = 64
INNER = 12
MIXED = 4
CHUNKS = RT // CHUNK
MESH = pl.DeviceIdType.MESH
F32 = jnp.float32
BF16 = jnp.bfloat16
I32 = jnp.int32


def iota(shape, dim):
    return lax.broadcasted_iota(I32, shape, dim)


def nn(a, b):
    return jnp.dot(a, b, preferred_element_type=F32)


def segments(keys, takes):
    square = (T, T)
    slot_row = iota(square, 0)
    slot_col = iota(square, 1)
    by_col = jnp.broadcast_to(keys, square)
    by_row = by_col.T
    take_row = jnp.broadcast_to(takes, square).T
    earlier_same = ((by_col == by_row) & (slot_col < slot_row)).astype(I32)
    lower = (by_col < by_row).astype(I32)
    rank = jnp.sum(earlier_same + lower, axis=1, keepdims=True)
    keep = (jnp.sum(earlier_same, axis=1, keepdims=True) > 0).astype(I32)
    at = rank == slot_col
    zero = jnp.zeros(square, I32)
    perm = jnp.sum(jnp.where(at, jnp.minimum(slot_row, SLOTS - 1), zero), axis=0, keepdims=True)
    take = jnp.sum(jnp.where(at, take_row, zero), axis=0, keepdims=True)
    kept = jnp.sum(jnp.where(at, jnp.broadcast_to(keep, square), zero), axis=0, keepdims=True)
    upto = jnp.sum((by_row <= slot_col).astype(I32), axis=0, keepdims=True)
    count = jnp.sum((by_row == slot_col).astype(I32), axis=0, keepdims=True)
    last = jnp.where(count > 0, upto, 0)
    return perm, take, kept, last


def kernel(
    signal_ref,
    time_weight_hbm,
    time_bias_hbm,
    mix_weight_hbm,
    mix_bias_hbm,
    tiles_hbm,
    rows_hbm,
    cols_hbm,
    count_hbm,
    out_ref,
    cur,
    lag,
    tiles,
    tiles_t,
    hidden,
    fwd,
    bwd,
    sums_f,
    sums_b,
    rim_out,
    rim_in,
    rim_out2,
    rim_in2,
    out,
    conv_w,
    mix_w,
    time_weight_ref,
    time_bias_ref,
    mix_weight_ref,
    mix_bias_ref,
    rows_ref,
    cols_ref,
    count_ref,
    table_v,
    table,
    local_sem,
    x_send,
    x_recv,
    r_send,
    r_recv,
    out_sem,
):
    region = lax.axis_index("region")
    tm = lax.axis_index("tm")
    regions = lax.axis_size("region")
    tms = lax.axis_size("tm")
    above, below = (region + 1, tm), (region - 1, tm)
    later, earlier = (region, tm + 1), (region, tm - 1)
    has_above, has_below = region < regions - 1, region > 0
    has_later, has_earlier = tm < tms - 1, tm > 0

    barrier = pltpu.get_barrier_semaphore()
    for there, peer in (
        (has_later, later),
        (has_earlier, earlier),
        (has_above, above),
        (has_below, below),
    ):

        @pl.when(there)
        def _(peer=peer):
            pl.semaphore_signal(barrier, inc=1, device_id=peer, device_id_type=MESH)

    loads = [
        pltpu.make_async_copy(src, dst, local_sem.at[index])
        for index, (src, dst) in enumerate(
            [
                (count_hbm, count_ref),
                (rows_hbm, rows_ref),
                (cols_hbm, cols_ref),
                (time_weight_hbm, time_weight_ref),
                (time_bias_hbm, time_bias_ref),
                (mix_weight_hbm, mix_weight_ref),
                (mix_bias_hbm, mix_bias_ref),
                (signal_ref, cur),
                (tiles_hbm, tiles),
            ]
        )
    ]
    for load in loads[:7]:
        load.start()
    peers = sum(
        there.astype(I32) for there in (has_later, has_earlier, has_above, has_below)
    )
    pl.semaphore_wait(barrier, peers)

    def columns(chunk):
        return pl.ds(chunk * (CHUNK * T), CHUNK * T)

    def shift(group, chunk):
        where = (pl.ds(group * ROWS, ROWS), columns(chunk))
        index = group * CHUNKS + chunk
        return pltpu.make_async_remote_copy(
            src_ref=signal_ref.at[where],
            dst_ref=lag.at[where],
            send_sem=x_send.at[index],
            recv_sem=x_recv.at[index],
            device_id=later,
            device_id_type=MESH,
        )

    order = [0, CHUNKS - 1] + list(range(1, CHUNKS - 1))

    @pl.when(has_later)
    def _():
        for group in range(GROUPS):
            for chunk in order:
                shift(group, chunk).start()

    @pl.when(jnp.logical_not(has_earlier))
    def _():
        lag[...] = jnp.zeros(lag.shape, BF16)

    @pl.when(jnp.logical_not(has_below))
    def _():
        for g in range(GROUPS):
            for ref, first in ((hidden[g], 0), (fwd[g], 0), (rim_in[g], 0), (rim_in2[g], 0)):
                ref[first : first + HB] = jnp.zeros((HB, ROWS, T), BF16)

    @pl.when(jnp.logical_not(has_above))
    def _():
        for g in range(GROUPS):
            for ref, first in (
                (hidden[g], HB + RT),
                (fwd[g], HB + RT),
                (rim_in[g], HB),
                (rim_in2[g], HB),
            ):
                ref[first : first + HB] = jnp.zeros((HB, ROWS, T), BF16)

    for load in loads[7:]:
        load.start()
    for load in loads[:7]:
        load.wait()

    spread = (lax.rem(iota((ROWS, CH), 0), CH) == iota((ROWS, CH), 1)).astype(BF16)
    same_day = iota((ROWS, ROWS), 0) // CH == iota((ROWS, ROWS), 1) // CH
    for part in range(2):
        tall = [nn(spread, time_weight_ref[tap]).astype(BF16) for tap in range(2)]
        pick = (
            iota((2 * CH, ROWS), 0) == part * CH + lax.rem(iota((2 * CH, ROWS), 1), CH)
        ).astype(BF16)
        for tap in range(2):
            wide = nn(tall[tap], pick).T * (1.0 if part == 0 else 0.5)
            conv_w[part * ROWS : (part + 1) * ROWS, tap * ROWS : (tap + 1) * ROWS] = jnp.where(
                same_day, wide, 0.0
            ).astype(BF16)
    tall_mix = nn(spread, mix_weight_ref[...]).astype(BF16)
    for branch in range(5):
        pick = (
            iota((5 * CH, ROWS), 0) == branch * CH + lax.rem(iota((5 * CH, ROWS), 1), CH)
        ).astype(BF16)
        mix_w[:, branch * ROWS : (branch + 1) * ROWS] = jnp.where(
            same_day, nn(tall_mix, pick), 0.0
        ).astype(BF16)
    channel = lax.rem(iota((ROWS, 1), 0), CH)

    def column_of(values, first):
        width = values.shape[1]
        hit = iota((ROWS, width), 1) == channel + first
        return jnp.sum(jnp.where(hit, jnp.broadcast_to(values, (ROWS, width)), 0.0), 1, keepdims=True)

    time_bias = time_bias_ref[...].reshape(1, 2 * CH)
    bias_filter = column_of(time_bias, 0)
    bias_gate = column_of(time_bias, CH) * 0.5
    bias_mix = column_of(mix_bias_ref[...].reshape(1, CH), 0)
    loads[7].wait()

    def to_region(src, dst, index, peer):
        return pltpu.make_async_remote_copy(
            src_ref=src,
            dst_ref=dst,
            send_sem=r_send.at[index],
            recv_sem=r_recv.at[index],
            device_id=peer,
            device_id_type=MESH,
        )

    def start_low(pair):
        pl.when(has_below)(pair[0].start)

    def start_high(pair):
        pl.when(has_above)(pair[1].start)

    def receive(pair):
        pl.when(has_above)(pair[0].wait_recv)
        pl.when(has_below)(pair[1].wait_recv)

    def sent(pair):
        pl.when(has_below)(pair[0].wait_send)
        pl.when(has_above)(pair[1].wait_send)

    def half_rows(h):
        return pl.ds(h * HALF, HALF)

    first_tiles, last_tiles = pl.ds(HB, HB), pl.ds(RT, HB)
    from_below, from_above = pl.ds(0, HB), pl.ds(HB + RT, HB)
    rim_first, rim_last = pl.ds(0, HB), pl.ds(HB, HB)
    halo, rim, edge, rim2 = [], [], [], []
    for g in range(GROUPS):
        base = 12 * g
        halo.append(
            (
                to_region(hidden[g].at[first_tiles], hidden[g].at[from_above], base, below),
                to_region(hidden[g].at[last_tiles], hidden[g].at[from_below], base + 1, above),
            )
        )
        rim.append(
            [
                (
                    to_region(
                        rim_out[g].at[rim_first, half_rows(h)],
                        rim_in[g].at[rim_last, half_rows(h)],
                        base + 2 + 6 * h,
                        below,
                    ),
                    to_region(
                        rim_out[g].at[rim_last, half_rows(h)],
                        rim_in[g].at[rim_first, half_rows(h)],
                        base + 3 + 6 * h,
                        above,
                    ),
                )
                for h in range(HALVES)
            ]
        )
        edge.append(
            (
                to_region(fwd[g].at[first_tiles], fwd[g].at[from_above], base + 4, below),
                to_region(fwd[g].at[last_tiles], fwd[g].at[from_below], base + 5, above),
            )
        )
        rim2.append(
            [
                (
                    to_region(
                        rim_out2[g].at[rim_first, half_rows(h)],
                        rim_in2[g].at[rim_last, half_rows(h)],
                        base + 6 + 4 * h,
                        below,
                    ),
                    to_region(
                        rim_out2[g].at[rim_last, half_rows(h)],
                        rim_in2[g].at[rim_first, half_rows(h)],
                        base + 7 + 4 * h,
                        above,
                    ),
                )
                for h in range(HALVES)
            ]
        )

    def gate(group, chunk):
        @pl.when(has_earlier)
        def _():
            shift(group, chunk).wait_recv()

        rows_here = pl.ds(group * ROWS, ROWS)

        def part(index, carry):
            first = chunk * CHUNK + index * PAIR
            where = pl.ds(pl.multiple_of(first * T, PAIR * T), PAIR * T)
            days = jnp.concatenate([lag[rows_here, where], cur[rows_here, where]], axis=0)
            pre = nn(conv_w[...], days)
            value = jnp.tanh(pre[:ROWS] + bias_filter) * (
                0.5 + 0.5 * jnp.tanh(pre[ROWS:] + bias_gate)
            )
            value = value.astype(BF16)
            for tile in range(PAIR):
                hidden[group][HB + first + tile] = value[:, tile * T : (tile + 1) * T]
            return carry

        lax.fori_loop(0, CHUNK // PAIR, part, 0, unroll=CHUNK // PAIR)

    def outer_gates(group):
        gate(group, 0)
        start_low(halo[group])
        gate(group, CHUNKS - 1)
        start_high(halo[group])

    def inner_gates(group):
        for chunk in range(1, CHUNKS - 1):
            gate(group, chunk)

    def extras(source, base, values, sums, first, start, count):
        here = pl.ds(start, count)

        def add(place, running):
            product = nn(
                source[table[first + 1, place] + base, here, :], values[table[first, place]]
            )
            running = jnp.where(table[first + 2, place] > 0, running, 0.0) + product
            sums[place + 1, here, :] = running
            return running

        lax.fori_loop(0, EXTRA, add, jnp.zeros((count, T), F32), unroll=UNROLL)

    def extras_f(g, source):
        extras(source, 0, tiles_t, sums_f[g], 0, 0, ROWS)

    def extras_b(g, source, base, h):
        extras(source, base, tiles, sums_b[g], 4, h * HALF, HALF)

    def rims(g, target, h):
        here = half_rows(h)

        def fill(tile, carry):
            target[tile, here, :] = sums_b[g][table[7, tile], here, :].astype(BF16)
            target[HB + tile, here, :] = sums_b[g][table[7, HB + RT + tile], here, :].astype(BF16)
            return carry

        lax.fori_loop(0, HB, fill, 0, unroll=HB)

    def forward(g, source, tile):
        return nn(source[HB + tile], tiles_t[tile]) + sums_f[g][table[3, tile]]

    def backward(g, source, base, tile):
        return nn(source[base + tile], tiles[tile]) + sums_b[g][table[7, HB + tile]]

    def hop_one(g):
        receive(halo[g])
        for h in range(HALVES):
            extras_b(g, hidden[g], HB, h)
            rims(g, rim_out[g], h)
            start_low(rim[g][h])
            start_high(rim[g][h])
        extras_f(g, hidden[g])

        def fwd_tile(tile, carry):
            fwd[g][HB + tile] = forward(g, hidden[g], tile).astype(BF16)
            return carry

        def fwd_rim(tile, carry):
            return fwd_tile(RT - HB + tile, fwd_tile(tile, carry))


        def inner(tile, carry):
            bwd[g][tile] = backward(g, hidden[g], HB, tile).astype(BF16)
            return fwd_tile(tile, carry)

        lax.fori_loop(HB, RT - HB, inner, 0, unroll=INNER)
        lax.fori_loop(0, HB, fwd_rim, 0, unroll=HB)
        start_low(edge[g])
        start_high(edge[g])

    def backward_two(g):
        for h in range(HALVES):
            here = half_rows(h)
            receive(rim[g][h])

            def bwd_rim(tile, carry):
                for at, arrived in ((tile, tile), (RT - HB + tile, HB + tile)):
                    total = nn(hidden[g][HB + at, here, :], tiles[at])
                    total = total + sums_b[g][table[7, HB + at], here, :]
                    total = total + rim_in[g][arrived, here, :].astype(F32)
                    bwd[g][at, here, :] = total.astype(BF16)
                return carry

            lax.fori_loop(0, HB, bwd_rim, 0, unroll=HB)
            extras_b(g, bwd[g], 0, h)
            rims(g, rim_out2[g], h)
            start_low(rim2[g][h])
            start_high(rim2[g][h])

    def mixed(g, first, received):
        columns_of_tiles = []
        for tile in range(PAIR):
            at = first + tile
            two = backward(g, bwd[g], 0, at)
            if received is not None:
                two = two + rim_in2[g][received + tile].astype(F32)
            columns_of_tiles.append(
                jnp.concatenate(
                    [
                        hidden[g][HB + at],
                        fwd[g][HB + at],
                        forward(g, fwd[g], at).astype(BF16),
                        bwd[g][at],
                        two.astype(BF16),
                    ],
                    axis=0,
                )
            )
        blocks = jnp.concatenate(columns_of_tiles, axis=1)
        rows_here = pl.ds(g * ROWS, ROWS)
        where = pl.ds(pl.multiple_of(first * T, PAIR * T), PAIR * T)
        total = nn(mix_w[...], blocks) + cur[rows_here, where].astype(F32) + bias_mix
        out[rows_here, where] = total.astype(BF16)

    def store(g, first, count, index):
        where = (pl.ds(g * ROWS, ROWS), pl.ds(first * T, count * T))
        return pltpu.make_async_copy(out.at[where], out_ref.at[where], out_sem.at[3 * g + index])

    stores = []

    def mix_inner(g):
        receive(edge[g])
        extras_f(g, fwd[g])

        def step(index, carry):
            mixed(g, HB + index * PAIR, None)
            return carry

        count = (RT - 2 * HB) // PAIR
        lax.fori_loop(0, count, step, 0, unroll=MIXED)
        stores.append(store(g, HB, RT - 2 * HB, 0))
        stores[-1].start()

    def mix_rim(g):
        for h in range(HALVES):
            receive(rim2[g][h])

        def step(index, carry):
            mixed(g, index * PAIR, index * PAIR)
            mixed(g, RT - HB + index * PAIR, HB + index * PAIR)
            return carry

        lax.fori_loop(0, HB // PAIR, step, 0, unroll=HB // PAIR)
        for first, index in ((0, 1), (RT - HB, 2)):
            stores.append(store(g, first, HB, index))
            stores[-1].start()

    outer_gates(0)

    lane = iota((1, T), 1)
    pad = jnp.zeros((1, T - SLOTS), I32)
    rows = jnp.concatenate([rows_ref[...], pad], axis=1)
    cols = jnp.concatenate([cols_ref[...], pad], axis=1)
    live = (lane >= RT) & (lane < count_ref[...])
    far = jnp.full((1, T), 2 * T, I32)
    perm_f, take_f, keep_f, last_f = segments(jnp.where(live, rows, far), cols)
    perm_b, take_b, keep_b, last_b = segments(jnp.where(live, cols, far), rows)
    table_v[...] = jnp.concatenate(
        [perm_f, take_f, keep_f, last_f, perm_b, take_b, keep_b, last_b], axis=0
    )
    to_scalars = pltpu.make_async_copy(table_v, table, local_sem.at[9])
    to_scalars.start()
    for g in range(GROUPS):
        sums_f[g][0] = jnp.zeros((ROWS, T), F32)
        sums_b[g][0] = jnp.zeros((ROWS, T), F32)

    loads[8].wait()

    def turn(slot, carry):
        tiles_t[slot] = tiles[slot].T
        return carry

    lax.fori_loop(0, SLOTS, turn, 0, unroll=16)
    to_scalars.wait()

    inner_gates(0)
    hop_one(0)
    backward_two(0)
    mix_inner(0)
    mix_rim(0)

    @pl.when(has_later)
    def _():
        for group in range(GROUPS):
            for chunk in range(CHUNKS):
                shift(group, chunk).wait_send()

    for group in range(GROUPS):
        for pair in (halo[group], edge[group], *rim[group], *rim2[group]):
            sent(pair)
    for copy in stores:
        copy.wait()


def hand_over(source, target, buffer, in_sem, out_sem):
    pieces = [pl.ds(index * 32, 32) for index in range(4)]
    arrive = [
        pltpu.make_async_copy(source.at[piece], buffer.at[piece], in_sem.at[index])
        for index, piece in enumerate(pieces)
    ]
    leave = [
        pltpu.make_async_copy(buffer.at[piece], target.at[piece], out_sem.at[index])
        for index, piece in enumerate(pieces)
    ]
    for copy in arrive:
        copy.start()
    for first, second in zip(arrive, leave):
        first.wait()
        second.start()
    for copy in leave:
        copy.wait()


def body(
    signal,
    time_weight,
    time_bias,
    mix_weight,
    mix_bias,
    tile_values,
    tile_rows,
    tile_cols,
    tile_count,
):
    width = signal.shape[2]
    whole = DAYS * CH
    hbm = pl.BlockSpec(memory_space=pltpu.HBM)
    panel = pltpu.VMEM((whole, width), BF16)

    def each(*shape):
        return [pltpu.VMEM(*shape) for _ in range(GROUPS)]

    result = pl.pallas_call(
        kernel,
        out_shape=jax.ShapeDtypeStruct((whole, width), BF16),
        in_specs=[hbm] * 9,
        out_specs=pl.BlockSpec(memory_space=pl.ANY),
        scratch_shapes=[
            panel,
            panel,
            pltpu.VMEM((SLOTS, T, T), BF16),
            pltpu.VMEM((SLOTS, T, T), BF16),
            each((RT + 2 * HB, ROWS, T), BF16),
            each((RT + 2 * HB, ROWS, T), BF16),
            each((RT, ROWS, T), BF16),
            each((EXTRA + 1, ROWS, T), F32),
            each((EXTRA + 1, ROWS, T), F32),
            each((2 * HB, ROWS, T), BF16),
            each((2 * HB, ROWS, T), BF16),
            each((2 * HB, ROWS, T), BF16),
            each((2 * HB, ROWS, T), BF16),
            panel,
            pltpu.VMEM((2 * ROWS, 2 * ROWS), BF16),
            pltpu.VMEM((ROWS, 5 * ROWS), BF16),
            pltpu.VMEM((2, CH, 2 * CH), BF16),
            pltpu.VMEM((2 * CH,), F32),
            pltpu.VMEM((CH, 5 * CH), BF16),
            pltpu.VMEM((CH,), F32),
            pltpu.VMEM((1, SLOTS), I32),
            pltpu.VMEM((1, SLOTS), I32),
            pltpu.VMEM((1, 1), I32),
            pltpu.VMEM((8, T), I32),
            pltpu.SMEM((8, T), I32),
            pltpu.SemaphoreType.DMA((10,)),
            pltpu.SemaphoreType.DMA((GROUPS * CHUNKS,)),
            pltpu.SemaphoreType.DMA((GROUPS * CHUNKS,)),
            pltpu.SemaphoreType.DMA((12 * GROUPS,)),
            pltpu.SemaphoreType.DMA((12 * GROUPS,)),
            pltpu.SemaphoreType.DMA((3 * GROUPS,)),
        ],
        compiler_params=pltpu.CompilerParams(
            collective_id=0, has_side_effects=True, vmem_limit_bytes=56 * 2**20
        ),
    )(
        signal.reshape(whole, width),
        jnp.transpose(time_weight, (0, 2, 1)),
        time_bias,
        mix_weight,
        mix_bias,
        tile_values[0],
        tile_rows,
        tile_cols,
        tile_count.reshape(1, 1),
    )
    anywhere = pl.BlockSpec(memory_space=pl.ANY)
    result = pl.pallas_call(
        hand_over,
        out_shape=jax.ShapeDtypeStruct((whole, width), BF16),
        in_specs=[anywhere],
        out_specs=anywhere,
        scratch_shapes=[
            panel,
            pltpu.SemaphoreType.DMA((4,)),
            pltpu.SemaphoreType.DMA((4,)),
        ],
        compiler_params=pltpu.CompilerParams(vmem_limit_bytes=56 * 2**20),
    )(result)
    return result.reshape(signal.shape)


def solution(mesh):
    placed = (
        P("tm", None, "region"),
        P(),
        P(),
        P(),
        P(),
        P("region", None, None, None),
        P("region", None),
        P("region", None),
        P("region"),
    )
    return jax.shard_map(
        body, mesh=mesh, in_specs=placed, out_specs=P("tm", None, "region"), check_vma=False
    )
```
